128 devices in a mesh: blk: 8 (over x_lo, y), head: 16 (over z, x_hi, core).
Axes of the slice: x: 4 (x_hi: 2, x_lo: 2; x = x_hi * 2 + x_lo), y: 4, z: 4, core: 2. Of those that a mesh axis runs over, the one named last changes fastest.
Arguments:
- queries: bfloat16 [16384, 4096], P(('blk', 'head')), may hold values from -13 to 13
- keys: bfloat16 [16384, 512], P(('blk', 'head')), may hold values from -13 to 13
- values: bfloat16 [16384, 512], P(('blk', 'head')), may hold values from -6 to 6
- positions: int32 [3, 16384], P(None, ('blk', 'head')), may hold values from 0 to 63
- block_order: int32 [16], replicated, may hold values from 0 to 15, each once
Outputs:
- attended: bfloat16 [16384, 4096], P(('blk', 'head'))
The draws below stay inside these ranges and needn't reach their ends.
All inputs are finite; a program needn't handle non-finite values.
Results may differ from the reference program's by a relative error of at most 0.006.
Values may be sent and summed in bfloat16 or wider, within the bound.
No kernel may reach another device: no remote copies, remote signals or barrier semaphores. Data moves between devices by JAX's collectives and lax.ppermute only.
A program may use at most 64 MiB of HBM per device.

```python
import math
import jax
import jax.numpy as jnp
from jax import lax

HD = 128
QH = 32
KVH = 4
TOKENS = 16384
N_BLK = 8


def draw_queries(key, part):
    key = jax.random.fold_in(key, 21)
    field = jnp.clip(jax.random.normal(key, (TOKENS, QH, HD), jnp.float32), -6.0, 6.0)
    return field.reshape(TOKENS, QH * HD).astype(jnp.bfloat16)


def draw_keys(key, part):
    key = jax.random.fold_in(key, 37)
    field = jnp.clip(jax.random.normal(key, (TOKENS, KVH, HD), jnp.float32), -6.0, 6.0)
    return field.reshape(TOKENS, KVH * HD).astype(jnp.bfloat16)


def set_ends(array, stream_key, least, largest):
    shape = array.shape
    spot = [jax.random.randint(jax.random.fold_in(stream_key, axis), (), 0, shape[axis]) for axis in range(len(shape))]
    array = array.at[tuple(spot)].set(least)
    longest = shape.index(max(shape))
    spot[longest] = (spot[longest] + 1) % shape[longest]
    return array.at[tuple(spot)].set(largest)


def shard_levels(key, shape, pieces, smallest, high):
    level = 1.0
    for position, parts in pieces:
        heights = jax.random.uniform(jax.random.fold_in(jax.random.fold_in(key, 6), position), (parts,), jnp.float32, smallest / len(pieces), high / len(pieces))
        level = level * jnp.repeat(jnp.exp(heights), shape[position] // parts).reshape((-1,) + (1,) * (len(shape) - 1 - position))
    return level


def normal_values(own_key, shape, deviation, limit, cuts=(), kind=jnp.bfloat16):
    array = jax.random.normal(own_key, shape, jnp.float32) * deviation
    if len(cuts) > 0:
        array = shard_levels(own_key, shape, cuts, -0.22, 0.18) * array
    return jnp.clip(array, min=-limit, max=limit).astype(kind)


def setup_inputs(seed: int = 0) -> dict:
    arg_keys = jax.random.split(jax.random.key(seed), 6)
    return {
        "queries": draw_queries(jax.random.fold_in(arg_keys[5], 71), 0),
        "keys": draw_keys(jax.random.fold_in(arg_keys[5], 71), 0),
        "values": normal_values(arg_keys[2], (TOKENS, KVH * HD), 1.0, 6.0, ((0, 128),)),
        "positions": set_ends(jax.random.randint(arg_keys[3], (3, TOKENS), 0, 64), jax.random.fold_in(arg_keys[3], 1), 0, 63).astype(jnp.int32),
        "block_order": jax.random.permutation(arg_keys[4], 2 * N_BLK).astype(jnp.int32),
    }


rope_base = 1000000.0

def rotate_heads(tensor, positions):
    head_dim = tensor.shape[-1]
    half_dim = head_dim // 2
    pair_index = jnp.arange(half_dim, dtype=jnp.int32)
    inverse = jnp.exp(pair_index.astype(jnp.float32) * (-2.0 * math.log(rope_base) / head_dim))
    first_end = head_dim // 8
    second_end = first_end + 3 * head_dim // 16
    picked = jnp.where(pair_index[None, :] < first_end, positions[0][:, None], jnp.where(pair_index[None, :] < second_end, positions[1][:, None], positions[2][:, None]))
    angles = picked.astype(jnp.float32) * inverse[None, :]
    cosine_table = jnp.cos(angles)[:, None, :]
    sine_table = jnp.sin(angles)[:, None, :]
    lower_half = tensor[..., :half_dim]
    upper_half = tensor[..., half_dim:]
    return jnp.concatenate([lower_half * cosine_table - upper_half * sine_table, upper_half * cosine_table + lower_half * sine_table], axis=-1)

def reference(queries, keys, values, positions, block_order):
    total_rows = queries.shape[0]
    block_count = block_order.shape[0]
    block_len = total_rows // block_count
    query_heads = queries.shape[1] // HD
    value_heads = keys.shape[1] // HD
    group_size = query_heads // value_heads
    scale = 1.0 / math.sqrt(HD)
    rot_queries = rotate_heads(queries.reshape(total_rows, query_heads, HD).astype(jnp.float32), positions).astype(jnp.bfloat16)
    rot_keys = rotate_heads(keys.reshape(total_rows, value_heads, HD).astype(jnp.float32), positions).astype(jnp.bfloat16)
    value_rows = values.reshape(total_rows, value_heads, HD)
    inverse_order = jnp.argsort(block_order).astype(jnp.int32)

    def to_sequence(tensor):
        shaped = tensor.reshape((block_count, block_len) + tensor.shape[1:])
        return shaped[inverse_order].reshape(tensor.shape)
    seq_queries = to_sequence(rot_queries)
    seq_keys = to_sequence(rot_keys)
    seq_values = to_sequence(value_rows)
    outputs = []
    for block_index in range(block_count):
        key_len = (block_index + 1) * block_len
        query_block = seq_queries[block_index * block_len:key_len]
        key_prefix = seq_keys[:key_len]
        value_prefix = seq_values[:key_len]
        query_pos = block_index * block_len + jnp.arange(block_len, dtype=jnp.int32)
        key_pos = jnp.arange(key_len, dtype=jnp.int32)
        allowed = key_pos[None, :] <= query_pos[:, None]

        def one_head(head_index):
            query_rows = lax.dynamic_index_in_dim(query_block, head_index, 1, keepdims=False)
            key_rows = lax.dynamic_index_in_dim(key_prefix, head_index // group_size, 1, keepdims=False)
            value_part = lax.dynamic_index_in_dim(value_prefix, head_index // group_size, 1, keepdims=False)
            scores = jnp.dot(query_rows, key_rows.T, preferred_element_type=jnp.float32) * scale
            scores = jnp.where(allowed, scores, -1e+30)
            peak = lax.optimization_barrier(jnp.max(scores, axis=1, keepdims=True))
            weights = jnp.where(allowed, jnp.exp(scores - peak), 0.0)
            total_weight = lax.optimization_barrier(jnp.sum(weights, axis=1, keepdims=True))
            mixed = jnp.dot(weights.astype(jnp.bfloat16), value_part, preferred_element_type=jnp.float32) / total_weight
            return mixed.astype(jnp.bfloat16)
        heads_out = lax.map(one_head, jnp.arange(query_heads, dtype=jnp.int32))
        outputs.append(jnp.transpose(heads_out, (1, 0, 2)).reshape(block_len, query_heads * HD))
    stacked = jnp.stack(outputs)[block_order]
    return stacked.reshape(total_rows, query_heads * HD)
```

```python
import functools
import math

import jax
import jax.numpy as jnp
from jax import lax
from jax.experimental import pallas as pl
from jax.experimental.pallas import tpu as pltpu
from jax.sharding import PartitionSpec as P

HD = 128
ROPE_BASE = 1000000.0
bf16 = jnp.bfloat16
f32 = jnp.float32
AXES = ("blk", "head")
NT = (((1,), (1,)), ((), ()))
NEG = -1e30
TILES = 4


def device_id(x, y, z, core):
    return ((x % 2) * 4 + y) * 16 + z * 4 + (x // 2) * 2 + core


COORDS = [(x, y, z, c) for x in range(4) for y in range(4) for z in range(4) for c in range(2)]
SPREAD_GROUPS = [
    [device_id(xh * 2 + b // 4, b % 4, z, c) for b in range(8) for z in range(4)]
    for xh in range(2)
    for c in range(2)
]


def ring_perm(first_axis_core, shift):
    pairs = []
    for x, y, z, c in COORDS:
        if c == first_axis_core:
            target = device_id(x, (y + shift) % 4, z, c)
        else:
            target = device_id((x + shift) % 4, y, z, c)
        pairs.append((device_id(x, y, z, c), target))
    return pairs


SWAP = [(device_id(x, y, z, c), device_id(x, y, z, 1 - c)) for x, y, z, c in COORDS]


def rope_tables(positions):
    pair = jnp.arange(HD // 2, dtype=jnp.int32)
    inverse = jnp.exp(pair.astype(f32) * (-2.0 * math.log(ROPE_BASE) / HD))
    picked = jnp.where(
        pair[None, :] < 16,
        positions[0][:, None],
        jnp.where(pair[None, :] < 40, positions[1][:, None], positions[2][:, None]),
    )
    angles = picked.astype(f32) * inverse[None, :]
    cos, sin = jnp.cos(angles), jnp.sin(angles)
    return jnp.concatenate([cos, cos], axis=1), jnp.concatenate([-sin, sin], axis=1)


def pack_kernel(q_ref, k_ref, v_ref, cos_ref, sin_ref, qo_ref, kvo_ref):
    cos, sin = cos_ref[...], sin_ref[...]
    fold = math.log2(math.e) / math.sqrt(HD)
    qcos, qsin = cos * fold, sin * fold

    def rotate(x, c, s):
        x = x.astype(f32)
        return (x * c + pltpu.roll(x, HD // 2, 1) * s).astype(bf16).reshape(8, 16, HD)

    for z in range(4):
        for h in range(8):
            col = (z * 8 + h) * HD
            qo_ref[:, z, :, h * HD : (h + 1) * HD] = rotate(q_ref[:, col : col + HD], qcos, qsin)
        kvo_ref[:, z, :, :HD] = rotate(k_ref[:, z * HD : (z + 1) * HD], cos, sin)
        kvo_ref[:, z, :, HD:] = v_ref[:, z * HD : (z + 1) * HD].reshape(8, 16, HD)


def pack(q, k, v, cos, sin):
    vmem = pl.BlockSpec(memory_space=pltpu.VMEM)
    return pl.pallas_call(
        pack_kernel,
        out_shape=(
            jax.ShapeDtypeStruct((8, 4, 16, 8 * HD), bf16),
            jax.ShapeDtypeStruct((8, 4, 16, 2 * HD), bf16),
        ),
        in_specs=[vmem] * 5,
        out_specs=(vmem, vmem),
        compiler_params=pltpu.CompilerParams(vmem_limit_bytes=24 * 2**20),
        name="pack",
    )(q, k, v, cos, sin)


def attend_kernel(inv, *refs, n_kv, first, last):
    refs = list(refs)
    q_ref = refs.pop(0)
    kv_refs = [refs.pop(0) for _ in range(n_kv)]
    kpos_ref, qpos_ref = refs.pop(0), refs.pop(0)
    if not first:
        acc_in, ml_in = refs.pop(0), refs.pop(0)
    if last:
        o_ref = refs.pop(0)
    else:
        acc_out, ml_out = refs.pop(0), refs.pop(0)
    m_ref, a_ref = refs
    pieces = sum(r.shape[0] for r in kv_refs)
    keys = pieces * 32
    per_unit = max(1, 1024 // keys)
    units = 2 if per_unit <= 2 else 1
    per_body = per_unit * units
    step = pl.program_id(0)
    base = step * TILES

    def query_tile(block):
        x = q_ref[block]
        return jnp.concatenate([x[:, h * HD : (h + 1) * HD] for h in range(8)], axis=0)

    def key_tile(orders):
        ks, vs = [], []
        for order in orders:
            block = inv[order]
            for r in kv_refs:
                kv = r[:, block].reshape(r.shape[0] * 32, 2 * HD)
                ks.append(kv[:, :HD])
                vs.append(kv[:, HD:])
        k = jnp.concatenate(ks, axis=0) if len(ks) > 1 else ks[0]
        v = jnp.concatenate(vs, axis=0) if len(vs) > 1 else vs[0]
        return k, jnp.concatenate([v, jnp.ones_like(v)], axis=1)

    rows = [pl.ds(w * 256, 256) for w in range(TILES)]
    for w in range(TILES):
        if first:
            m_ref[rows[w], :] = jnp.full((256, HD), NEG, f32)
            a_ref[rows[w], :] = jnp.zeros((256, 2 * HD), f32)
        else:
            ml = ml_in[w]
            m_ref[rows[w], :] = jnp.broadcast_to(ml[:, :1], (256, HD))
            a_ref[rows[w], :HD] = acc_in[w]
            a_ref[rows[w], HD:] = jnp.broadcast_to(ml[:, HD - 1 :], (256, HD))
    queries = [query_tile(inv[base + w]) for w in range(TILES)]

    def scores(w, tile, masked):
        s = lax.dot_general(queries[w], tile[0], NT, preferred_element_type=f32)
        if masked:
            allowed = jnp.tile(kpos_ref[...], (256, 1)) <= jnp.tile(qpos_ref[...], (1, keys // HD))
            own = jnp.where(allowed, s[:, s.shape[1] - keys :], NEG)
            s = jnp.concatenate([s[:, : s.shape[1] - keys], own], axis=1) if s.shape[1] > keys else own
        return s

    def weigh(w, s):
        before = m_ref[rows[w], :]
        peak = jnp.maximum(before, jnp.max(s, axis=1, keepdims=True))
        p = jnp.exp2(s - jnp.tile(peak, (1, s.shape[1] // HD))).astype(bf16)
        m_ref[rows[w], :] = peak
        return p, jnp.exp2(before - peak)

    def add(w, p, factor, vext):
        o = jnp.dot(p, vext, preferred_element_type=f32)
        a_ref[rows[w], :] = a_ref[rows[w], :] * jnp.tile(factor, (1, 2)) + o

    def run(todo):
        ahead = scores(*todo[0])
        pending = None
        for i, (w, tile, _) in enumerate(todo):
            s = ahead
            if i + 1 < len(todo):
                ahead = scores(*todo[i + 1])
            p, factor = weigh(w, s)
            if pending is not None:
                add(*pending)
            pending = (w, p, factor, tile[1])
        add(*pending)

    def body(j, carry):
        tiles = [
            key_tile([j * per_body + u * per_unit + i for i in range(per_unit)])
            for u in range(units)
        ]
        run([(w, t, False) for t in tiles for w in range(TILES)])
        return carry

    lax.fori_loop(0, base // per_body, body, 0)

    todo = []
    for w in range(TILES):
        for start in range(0, w + 1, per_unit):
            stop = min(start + per_unit, w + 1)
            todo.append((w, key_tile([base + i for i in range(start, stop)]), stop == w + 1))
    run(todo)

    for w in range(TILES):
        a = a_ref[rows[w], :]
        if last:
            o = (a[:, :HD] / a[:, HD:]).astype(bf16)
            block = inv[base + w]
            for h in range(8):
                o_ref[block, :, h * HD : (h + 1) * HD] = o[h * 32 : (h + 1) * 32]
        else:
            acc_out[w] = a[:, :HD]
            lane = lax.broadcasted_iota(jnp.int32, (256, HD), 1)
            ml_out[w] = jnp.where(lane < HD // 2, m_ref[rows[w], :], a[:, HD:])


def attend(inv, q, kvs, kpos, qpos, state, last, name):
    first = state is None

    def whole(x):
        return pl.BlockSpec(x.shape, lambda i, inv: (0,) * x.ndim, pipeline_mode=pl.Buffered(1))

    part = pl.BlockSpec((TILES, 256, HD), lambda i, inv: (i, 0, 0))
    operands = [q, *kvs, kpos, qpos]
    in_specs = [whole(x) for x in operands]
    if not first:
        operands += list(state)
        in_specs += [part, part]
    full = jax.ShapeDtypeStruct((16, 256, HD), f32)
    pieces = sum(x.shape[0] for x in kvs)
    work = 17 * 16 // 2 * 256 * 32 * pieces
    return pl.pallas_call(
        functools.partial(attend_kernel, n_kv=len(kvs), first=first, last=last),
        out_shape=jax.ShapeDtypeStruct(q.shape, bf16) if last else (full, full),
        grid_spec=pltpu.PrefetchScalarGridSpec(
            num_scalar_prefetch=1,
            grid=(16 // TILES,),
            in_specs=in_specs,
            out_specs=whole(q) if last else (part, part),
            scratch_shapes=[
                pltpu.VMEM((TILES * 256, HD), f32),
                pltpu.VMEM((TILES * 256, 2 * HD), f32),
            ],
        ),
        compiler_params=pltpu.CompilerParams(vmem_limit_bytes=48 * 2**20),
        cost_estimate=pl.CostEstimate(
            flops=work * 1024, bytes_accessed=8 * 2**20, transcendentals=work
        ),
        name=name,
    )(inv, *operands)


def per_device(queries, keys, values, positions, block_order):
    blk, head = lax.axis_index("blk"), lax.axis_index("head")
    core = head % 2
    x = (head // 2) % 2 * 2 + blk // 4
    y = blk % 4

    def offsets(px, py, pc):
        start = ((px // 2) * 2 + pc) * 128 + ((px % 2) * 4 + py) * 16
        return jnp.concatenate([start + jnp.arange(16), start + 512 + jnp.arange(16)]).astype(jnp.int32)

    cos, sin = rope_tables(positions)
    q_send, kv_send = pack(queries, keys, values, cos, sin)
    inv = jnp.sum(
        jnp.where(
            block_order[None, :] == jnp.arange(16, dtype=jnp.int32)[:, None],
            jnp.arange(16, dtype=jnp.int32)[None, :],
            0,
        ),
        axis=1,
    ).astype(jnp.int32)

    def spread(t):
        return lax.all_to_all(t, AXES, 0, 0, axis_index_groups=SPREAD_GROUPS)

    own = spread(kv_send.reshape(32, 16, 2 * HD)).reshape(16, 32, 2 * HD)
    q = spread(q_send.reshape(32, 16, 8 * HD)).reshape(16, 32, 8 * HD)
    qpos = jnp.broadcast_to(jnp.tile(offsets(x, y, core), 8)[:, None], (256, HD))

    send = lambda t, perm: lax.ppermute(t, AXES, perm)
    plus1, minus1 = ring_perm(0, 1), ring_perm(0, -1)
    plus2, minus2 = ring_perm(1, 1), ring_perm(1, -1)

    from_minus = send(own, plus1)
    from_plus = send(own, minus1)
    far = jnp.concatenate(
        [send(from_minus[:, :16], plus1), send(from_plus[:, 16:], minus1)], axis=1
    )
    line = jnp.stack([own, from_minus, from_plus, far])
    line_other = send(line, SWAP)
    shifts = [0, -1, 1, 2]

    def line_offsets(dx, dy, c):
        return jnp.concatenate(
            [
                offsets(
                    (x + dx + jnp.where(c == 0, 0, s)) % 4,
                    (y + dy + jnp.where(c == 0, s, 0)) % 4,
                    c,
                )
                for s in shifts
            ]
        )

    def moved_offsets(shift, c):
        return line_offsets(jnp.where(c == 0, shift, 0), jnp.where(c == 0, 0, shift), c)

    line_minus = send(line, plus2)
    line_plus = send(line, minus2)
    far_a = send(line_minus[:2], plus2)
    far_b = send(line_plus[2:], minus2)
    minus_other, plus_other = send(line_minus, SWAP), send(line_plus, SWAP)
    far_a_other, far_b_other = send(far_a, SWAP), send(far_b, SWAP)

    other = 1 - core
    kpos1 = jnp.concatenate([moved_offsets(0, core), moved_offsets(0, other)])[None]
    kpos2 = jnp.concatenate([moved_offsets(-1, core), moved_offsets(1, core)])[None]
    far_own, far_other = moved_offsets(2, core), moved_offsets(2, other)
    kpos3 = jnp.concatenate(
        [moved_offsets(-1, other), moved_offsets(1, other), far_own, far_other]
    )[None]

    state = attend(inv, q, [line, line_other], kpos1, qpos, None, False, "attend_near")
    state = attend(inv, q, [line_minus, line_plus], kpos2, qpos, state, False, "attend_next")
    mixed = attend(
        inv,
        q,
        [minus_other, plus_other, far_a, far_b, far_a_other, far_b_other],
        kpos3,
        qpos,
        state,
        True,
        "attend_far",
    )
    back = spread(mixed.reshape(32, 16, 8 * HD)).reshape(8, 4, 16, 8 * HD)
    return jnp.transpose(back, (0, 2, 1, 3)).reshape(128, 32 * HD)


def solution(mesh):
    return jax.shard_map(
        per_device,
        mesh=mesh,
        in_specs=(P(AXES, None), P(AXES, None), P(AXES, None), P(None, AXES), P()),
        out_specs=P(AXES, None),
        check_vma=False,
    )
```

```python
import functools
import math

import jax
import jax.numpy as jnp
import numpy as np
from jax import lax
from jax.experimental import pallas as pl
from jax.experimental.pallas import tpu as pltpu
from jax.sharding import PartitionSpec as P

HD = 128
ROPE_BASE = 1000000.0
bf16 = jnp.bfloat16
f32 = jnp.float32
AXES = ("blk", "head")
NT = (((1,), (1,)), ((), ()))
NEG = -1e30
TILES = 4
VMEM_LIMIT = 60 * 2**20


def device_id(x, y, z, core):
    return ((x % 2) * 4 + y) * 16 + z * 4 + (x // 2) * 2 + core


COORDS = [(x, y, z, c) for x in range(4) for y in range(4) for z in range(4) for c in range(2)]
SPREAD_GROUPS = [
    [device_id(xh * 2 + b // 4, b % 4, z, c) for b in range(8) for z in range(4)]
    for xh in range(2)
    for c in range(2)
]


def ring_perm(first_axis_core, shift):
    pairs = []
    for x, y, z, c in COORDS:
        if c == first_axis_core:
            target = device_id(x, (y + shift) % 4, z, c)
        else:
            target = device_id((x + shift) % 4, y, z, c)
        pairs.append((device_id(x, y, z, c), target))
    return pairs


SHIFTS = (0, -1, 1, 2)


def row_offsets(x, y, c):
    start = ((x % 4) // 2 * 2 + c) * 128 + ((x % 2) * 4 + y % 4) * 16
    return [start + half * 512 + r for half in range(2) for r in range(16)]


def line_offsets(x, y, c, shift):
    if c == 0:
        return [o for s in SHIFTS for o in row_offsets(x + shift, y + s, c)]
    return [o for s in SHIFTS for o in row_offsets(x + s, y + shift, c)]


def key_offsets(parts):
    table = np.zeros((128, 1, 128 * len(parts)), np.int32)
    for x, y, z, c in COORDS:
        row = [o for shift, own in parts for o in line_offsets(x, y, c if own else 1 - c, shift)]
        table[device_id(x, y, z, c), 0] = row
    return table


KEY_OFFSETS = [
    key_offsets([(0, True), (0, False)]),
    key_offsets([(-1, True), (1, True)]),
    key_offsets([(-1, False), (1, False), (2, True), (2, False)]),
]
SWAP = [(device_id(x, y, z, c), device_id(x, y, z, 1 - c)) for x, y, z, c in COORDS]


def rope_tables(positions):
    pair = jnp.arange(HD // 2, dtype=jnp.int32)
    inverse = jnp.exp(pair.astype(f32) * (-2.0 * math.log(ROPE_BASE) / HD))
    picked = jnp.where(
        pair[None, :] < 16,
        positions[0][:, None],
        jnp.where(pair[None, :] < 40, positions[1][:, None], positions[2][:, None]),
    )
    angles = picked.astype(f32) * inverse[None, :]
    cos, sin = jnp.cos(angles), jnp.sin(angles)
    return jnp.concatenate([cos, cos], axis=1), jnp.concatenate([-sin, sin], axis=1)


def pack_kernel(q_ref, k_ref, v_ref, cos_ref, sin_ref, out_ref):
    cos, sin = cos_ref[...], sin_ref[...]
    fold = math.log2(math.e) / math.sqrt(HD)
    qcos, qsin = cos * fold, sin * fold

    def rotate(x, c, s):
        x = x.astype(f32)
        return (x * c + pltpu.roll(x, HD // 2, 1) * s).astype(bf16).reshape(8, 16, HD)

    for h in range(8):
        cols = slice(h * HD, (h + 1) * HD)
        out_ref[:, 0, :, cols] = rotate(q_ref[:, cols], qcos, qsin)
    out_ref[:, 0, :, 8 * HD : 9 * HD] = rotate(k_ref[...], cos, sin)
    out_ref[:, 0, :, 9 * HD :] = v_ref[...].reshape(8, 16, HD)


def pack(q, k, v, cos, sin):
    table = pl.BlockSpec((128, HD), lambda z: (0, 0))
    small = pl.BlockSpec((128, HD), lambda z: (0, z))
    return pl.pallas_call(
        pack_kernel,
        out_shape=jax.ShapeDtypeStruct((8, 4, 16, 10 * HD), bf16),
        grid=(4,),
        in_specs=[pl.BlockSpec((128, 8 * HD), lambda z: (0, z)), small, small, table, table],
        out_specs=pl.BlockSpec((8, 1, 16, 10 * HD), lambda z: (0, z, 0, 0)),
        compiler_params=pltpu.CompilerParams(vmem_limit_bytes=VMEM_LIMIT),
        name="pack",
    )(q, k, v, cos, sin)


def unpack_kernel(x_ref, o_ref):
    o_ref[...] = x_ref[:, 0].reshape(128, 8 * HD)


def unpack(x):
    return pl.pallas_call(
        unpack_kernel,
        out_shape=jax.ShapeDtypeStruct((128, 32 * HD), bf16),
        grid=(4,),
        in_specs=[pl.BlockSpec((8, 1, 16, 8 * HD), lambda z: (0, z, 0, 0))],
        out_specs=pl.BlockSpec((128, 8 * HD), lambda z: (0, z)),
        compiler_params=pltpu.CompilerParams(vmem_limit_bytes=VMEM_LIMIT),
        name="unpack",
    )(x)


def attend_kernel(inv, *refs, n_kv, first, last):
    refs = list(refs)
    q_refs = [refs.pop(0) for _ in range(TILES)]
    kv_hbm = [refs.pop(0) for _ in range(n_kv)]
    kpos_ref = refs.pop(0)
    if not first:
        acc_in, ml_in = refs.pop(0), refs.pop(0)
    if last:
        o_hbm = refs.pop(0)
    else:
        acc_out, ml_out = refs.pop(0), refs.pop(0)
    m_ref, a_ref = refs.pop(0), refs.pop(0)
    kv_refs = [refs.pop(0) for _ in range(n_kv)]
    kv_sem = refs.pop(0)
    if last:
        o_ref, o_sem = refs
    pieces = sum(r.shape[0] for r in kv_refs)
    keys = pieces * 32
    per_unit = max(1, 1024 // keys)
    units = 2 if per_unit <= 2 else 1
    per_body = per_unit * units
    step = pl.program_id(0)
    base = step * TILES

    def fetch(i, order):
        block = inv[order]
        return pltpu.make_async_copy(
            kv_hbm[i].at[:, block], kv_refs[i].at[:, block], kv_sem.at[i, order]
        )

    def start_fetch(begin):
        for w in range(TILES):
            for i in range(n_kv):
                fetch(i, begin + w).start()

    @pl.when(step == 0)
    def _():
        start_fetch(0)

    @pl.when(step < 16 // TILES - 1)
    def _():
        start_fetch(base + TILES)

    def query_tile(ref):
        x = ref[0]
        return jnp.concatenate([x[:, h * HD : (h + 1) * HD] for h in range(8)], axis=0)

    def key_tile(orders):
        ks, vs = [], []
        for order in orders:
            block = inv[order]
            for r in kv_refs:
                kv = r[:, block].reshape(r.shape[0] * 32, 2 * HD)
                ks.append(kv[:, :HD])
                vs.append(kv[:, HD:])
        k = jnp.concatenate(ks, axis=0) if len(ks) > 1 else ks[0]
        v = jnp.concatenate(vs, axis=0) if len(vs) > 1 else vs[0]
        return k, jnp.concatenate([v, jnp.ones_like(v)], axis=1)

    rows = [pl.ds(w * 256, 256) for w in range(TILES)]
    for w in range(TILES):
        if first:
            m_ref[rows[w], :] = jnp.full((256, HD), NEG, f32)
            a_ref[rows[w], :] = jnp.zeros((256, 2 * HD), f32)
        else:
            ml = ml_in[w]
            m_ref[rows[w], :] = jnp.broadcast_to(ml[:, :1], (256, HD))
            a_ref[rows[w], :HD] = acc_in[w]
            a_ref[rows[w], HD:] = jnp.broadcast_to(ml[:, HD - 1 :], (256, HD))
    queries = [query_tile(r) for r in q_refs]

    def scores(w, tile, masked):
        s = lax.dot_general(queries[w], tile[0], NT, preferred_element_type=f32)
        if masked:
            row = lax.broadcasted_iota(jnp.int32, (256, HD), 0)
            device = inv[16]
            start = (device % 4) * 128 + (device // 16) * 16
            qpos = start + (row // 16 % 2) * 512 + row % 16
            allowed = jnp.tile(kpos_ref[0], (256, 1)) <= jnp.tile(qpos, (1, keys // HD))
            own = jnp.where(allowed, s[:, s.shape[1] - keys :], NEG)
            s = jnp.concatenate([s[:, : s.shape[1] - keys], own], axis=1) if s.shape[1] > keys else own
        return s

    def weigh(w, s):
        before = m_ref[rows[w], :]
        peak = jnp.maximum(before, jnp.max(s, axis=1, keepdims=True))
        p = jnp.exp2(s - jnp.tile(peak, (1, s.shape[1] // HD))).astype(bf16)
        m_ref[rows[w], :] = peak
        return p, jnp.exp2(before - peak)

    def add(w, p, factor, vext):
        o = jnp.dot(p, vext, preferred_element_type=f32)
        a_ref[rows[w], :] = a_ref[rows[w], :] * jnp.tile(factor, (1, 2)) + o

    def run(todo):
        ahead = scores(*todo[0])
        pending = None
        for i, (w, tile, _) in enumerate(todo):
            s = ahead
            if i + 1 < len(todo):
                ahead = scores(*todo[i + 1])
            p, factor = weigh(w, s)
            if pending is not None:
                add(*pending)
            pending = (w, p, factor, tile[1])
        add(*pending)

    def body(j, carry):
        tiles = [
            key_tile([j * per_body + u * per_unit + i for i in range(per_unit)])
            for u in range(units)
        ]
        run([(w, t, False) for t in tiles for w in range(TILES)])
        return carry

    lax.fori_loop(0, base // per_body, body, 0)

    for w in range(TILES):
        for i in range(n_kv):
            fetch(i, base + w).wait()
    todo = []
    for w in range(TILES):
        for start in range(0, w + 1, per_unit):
            stop = min(start + per_unit, w + 1)
            todo.append((w, key_tile([base + i for i in range(start, stop)]), stop == w + 1))
    run(todo)

    def store(order):
        block = inv[order]
        return pltpu.make_async_copy(o_ref.at[block], o_hbm.at[block], o_sem.at[order])

    for w in range(TILES):
        a = a_ref[rows[w], :]
        if last:
            o = (a[:, :HD] / a[:, HD:]).astype(bf16)
            block = inv[base + w]
            for h in range(8):
                o_ref[block, :, h * HD : (h + 1) * HD] = o[h * 32 : (h + 1) * 32]
            store(base + w).start()
        else:
            acc_out[w] = a[:, :HD]
            lane = lax.broadcasted_iota(jnp.int32, (256, HD), 1)
            ml_out[w] = jnp.where(lane < HD // 2, m_ref[rows[w], :], a[:, HD:])
    if last:

        @pl.when(step == 16 // TILES - 1)
        def _():
            for order in range(16):
                store(order).wait()


def attend(inv, q, kvs, kpos, state, last, name):
    first = state is None

    own_row = pl.BlockSpec((1, 1, kpos.shape[2]), lambda i, inv: (inv[16], 0, 0))

    def query_spec(w):
        return pl.BlockSpec((1, 32, 8 * HD), lambda i, inv: (inv[i * TILES + w], 0, 0))

    hbm = pl.BlockSpec(memory_space=pl.ANY)
    part = pl.BlockSpec((TILES, 256, HD), lambda i, inv: (i, 0, 0))
    operands = [q] * TILES + [*kvs, kpos]
    in_specs = [query_spec(w) for w in range(TILES)] + [hbm] * len(kvs) + [own_row]
    if not first:
        operands += list(state)
        in_specs += [part, part]
    full = jax.ShapeDtypeStruct((16, 256, HD), f32)
    mixed = jax.ShapeDtypeStruct((16, 32, 8 * HD), bf16)
    pieces = sum(x.shape[0] for x in kvs)
    work = 17 * 16 // 2 * 256 * 32 * pieces
    scratch = [
        pltpu.VMEM((TILES * 256, HD), f32),
        pltpu.VMEM((TILES * 256, 2 * HD), f32),
        *[pltpu.VMEM(x.shape, bf16) for x in kvs],
        pltpu.SemaphoreType.DMA((len(kvs), 16)),
    ]
    if last:
        scratch += [pltpu.VMEM(mixed.shape, bf16), pltpu.SemaphoreType.DMA((16,))]
    return pl.pallas_call(
        functools.partial(attend_kernel, n_kv=len(kvs), first=first, last=last),
        out_shape=mixed if last else (full, full),
        grid_spec=pltpu.PrefetchScalarGridSpec(
            num_scalar_prefetch=1,
            grid=(16 // TILES,),
            in_specs=in_specs,
            out_specs=hbm if last else (part, part),
            scratch_shapes=scratch,
        ),
        compiler_params=pltpu.CompilerParams(vmem_limit_bytes=VMEM_LIMIT),
        cost_estimate=pl.CostEstimate(
            flops=work * 1024, bytes_accessed=8 * 2**20, transcendentals=work
        ),
        name=name,
    )(inv, *operands)


def per_device(queries, keys, values, positions, block_order):
    cos, sin = rope_tables(positions)
    packed = pack(queries, keys, values, cos, sin)
    inv = jnp.sum(
        jnp.where(
            block_order[None, :] == jnp.arange(16, dtype=jnp.int32)[:, None],
            jnp.arange(16, dtype=jnp.int32)[None, :],
            0,
        ),
        axis=1,
    ).astype(jnp.int32)
    inv = jnp.concatenate([inv, lax.axis_index(AXES).astype(jnp.int32)[None]])

    def spread(t):
        return lax.all_to_all(t, AXES, 0, 0, axis_index_groups=SPREAD_GROUPS)

    q = spread(packed.reshape(32, 16, 10 * HD)).reshape(16, 32, 10 * HD)
    own = q[:, :, 8 * HD :]
    send = lambda t, perm: lax.ppermute(t, AXES, perm)
    plus1, minus1 = ring_perm(0, 1), ring_perm(0, -1)
    plus2, minus2 = ring_perm(1, 1), ring_perm(1, -1)

    from_minus = send(own, plus1)
    from_plus = send(own, minus1)
    far = jnp.concatenate(
        [send(from_minus[:, :16], plus1), send(from_plus[:, 16:], minus1)], axis=1
    )
    line = jnp.stack([own, from_minus, from_plus, far])
    line_other = send(line, SWAP)
    line_minus = send(line, plus2)
    line_plus = send(line, minus2)
    state = attend(inv, q, [line, line_other], KEY_OFFSETS[0], None, False, "attend_near")
    line_minus, line_plus, state = lax.optimization_barrier((line_minus, line_plus, state))
    far_a = send(line_minus[:2], plus2)
    far_b = send(line_plus[2:], minus2)
    minus_other, plus_other = send(line_minus, SWAP), send(line_plus, SWAP)
    state = attend(inv, q, [line_minus, line_plus], KEY_OFFSETS[1], state, False, "attend_next")
    far_a, far_b, state = lax.optimization_barrier((far_a, far_b, state))
    far_a_other, far_b_other = send(far_a, SWAP), send(far_b, SWAP)
    mixed = attend(
        inv,
        q,
        [minus_other, plus_other, far_a, far_b, far_a_other, far_b_other],
        KEY_OFFSETS[2],
        state,
        True,
        "attend_far",
    )
    back = spread(mixed.reshape(32, 16, 8 * HD)).reshape(8, 4, 16, 8 * HD)
    return unpack(back)


def solution(mesh):
    return jax.shard_map(
        per_device,
        mesh=mesh,
        in_specs=(P(AXES, None), P(AXES, None), P(AXES, None), P(None, AXES), P()),
        out_specs=P(AXES, None),
        check_vma=False,
    )
```

```python
import functools
import math

import jax
import jax.numpy as jnp
import numpy as np
from jax import lax
from jax.experimental import pallas as pl
from jax.experimental.pallas import tpu as pltpu
from jax.sharding import PartitionSpec as P

HD = 128
ROPE_BASE = 1000000.0
bf16 = jnp.bfloat16
f32 = jnp.float32
AXES = ("blk", "head")
NT = (((1,), (1,)), ((), ()))
NEG = -1e30
CHAINS = 4
VMEM_LIMIT = 24 * 2**20


def device_id(x, y, z, core):
    return ((x % 2) * 4 + y) * 16 + z * 4 + (x // 2) * 2 + core


COORDS = [(x, y, z, c) for x in range(4) for y in range(4) for z in range(4) for c in range(2)]
SPREAD_GROUPS = [
    [device_id(xh * 2 + b // 4, b % 4, z, c) for b in range(8) for z in range(4)]
    for xh in range(2)
    for c in range(2)
]


def ring_perm(first_axis_core, shift):
    pairs = []
    for x, y, z, c in COORDS:
        if c == first_axis_core:
            target = device_id(x, (y + shift) % 4, z, c)
        else:
            target = device_id((x + shift) % 4, y, z, c)
        pairs.append((device_id(x, y, z, c), target))
    return pairs


SHIFTS = (0, -1, 1, 2)


def row_offsets(x, y, c):
    start = ((x % 4) // 2 * 2 + c) * 128 + ((x % 2) * 4 + y % 4) * 16
    return [start + half * 512 + r for half in range(2) for r in range(16)]


def line_offsets(x, y, c, shift):
    if c == 0:
        return [o for s in SHIFTS for o in row_offsets(x + shift, y + s, c)]
    return [o for s in SHIFTS for o in row_offsets(x + s, y + shift, c)]


def key_offsets(parts):
    table = np.zeros((128, 128 * len(parts)), np.int32)
    for x, y, z, c in COORDS:
        row = [o for shift, own in parts for o in line_offsets(x, y, c if own else 1 - c, shift)]
        table[device_id(x, y, z, c)] = row
    return table


KEY_OFFSETS = key_offsets(
    [(0, True), (0, False)]
    + [(-1, True), (1, True)]
    + [(-1, False), (1, False), (2, True), (2, False)]
)
SWAP = [(device_id(x, y, z, c), device_id(x, y, z, 1 - c)) for x, y, z, c in COORDS]


def rope_tables(pos_ref):
    lane = lax.broadcasted_iota(jnp.int32, (128, HD), 1) % (HD // 2)
    inverse = jnp.exp(lane.astype(f32) * (-2.0 * math.log(ROPE_BASE) / HD))
    columns = [
        jnp.transpose(jnp.broadcast_to(pos_ref[i : i + 1, :].astype(f32), (128, 128)))
        for i in range(3)
    ]
    angles = jnp.where(lane < 16, columns[0], jnp.where(lane < 40, columns[1], columns[2])) * inverse
    upper = lax.broadcasted_iota(jnp.int32, (128, HD), 1) >= HD // 2
    sin = jnp.sin(angles)
    return jnp.cos(angles), jnp.where(upper, sin, -sin)


def pack_kernel(q_hbm, k_hbm, v_hbm, pos_ref, out_ref, q_ref, k_ref, v_ref, sem):
    copies = [
        pltpu.make_async_copy(k_hbm, k_ref, sem.at[4]),
        pltpu.make_async_copy(v_hbm, v_ref, sem.at[5]),
    ]
    for z in range(4):
        cols = pl.ds(z * 8 * HD, 8 * HD)
        copies.append(pltpu.make_async_copy(q_hbm.at[:, cols], q_ref.at[:, cols], sem.at[z]))
    for c in copies:
        c.start()
    cos, sin = rope_tables(pos_ref)
    fold = math.log2(math.e) / math.sqrt(HD)
    qcos, qsin = cos * fold, sin * fold

    def rotate(x, c, s):
        x = x.astype(f32)
        return (x * c + pltpu.roll(x, HD // 2, 1) * s).astype(bf16).reshape(8, 16, HD)

    copies[0].wait()
    copies[1].wait()
    for z in range(4):
        cols = slice(z * HD, (z + 1) * HD)
        out_ref[:, z, :, 8 * HD : 9 * HD] = rotate(k_ref[:, cols], cos, sin)
        out_ref[:, z, :, 9 * HD :] = v_ref[:, cols].reshape(8, 16, HD)
    for z in range(4):
        copies[2 + z].wait()
        for h in range(8):
            col = (z * 8 + h) * HD
            out_ref[:, z, :, h * HD : (h + 1) * HD] = rotate(q_ref[:, col : col + HD], qcos, qsin)


VMEM = pl.BlockSpec(memory_space=pltpu.VMEM)
HBM = pl.BlockSpec(memory_space=pltpu.HBM)
SMEM = pl.BlockSpec(memory_space=pltpu.SMEM)


def pack(q, k, v, positions):
    return pl.pallas_call(
        pack_kernel,
        out_shape=jax.ShapeDtypeStruct((8, 4, 16, 10 * HD), bf16),
        in_specs=[HBM, HBM, HBM, VMEM],
        out_specs=VMEM,
        scratch_shapes=[
            pltpu.VMEM(q.shape, bf16),
            pltpu.VMEM(k.shape, bf16),
            pltpu.VMEM(v.shape, bf16),
            pltpu.SemaphoreType.DMA((6,)),
        ],
        compiler_params=pltpu.CompilerParams(vmem_limit_bytes=VMEM_LIMIT),
        name="pack",
    )(q, k, v, positions)


def unpack_kernel(*refs):
    *parts, o_hbm, sem = refs
    width = parts[0].shape[3]
    copies = [
        pltpu.make_async_copy(
            part.at[:, z],
            o_hbm.at[:, :, pl.ds((z * len(parts) + i) * width, width)],
            sem.at[i, z],
        )
        for i, part in enumerate(parts)
        for z in range(4)
    ]
    for c in copies:
        c.start()
    for c in copies:
        c.wait()


def unpack(parts):
    out = pl.pallas_call(
        unpack_kernel,
        out_shape=jax.ShapeDtypeStruct((8, 16, 32 * HD), bf16),
        in_specs=[VMEM] * len(parts),
        out_specs=HBM,
        scratch_shapes=[pltpu.SemaphoreType.DMA((len(parts), 4))],
        compiler_params=pltpu.CompilerParams(vmem_limit_bytes=VMEM_LIMIT),
        name="unpack",
    )(*parts)
    return out.reshape(128, 32 * HD)


def attend_kernel(meta, *refs, n_kv, first, last, heads):
    refs = list(refs)
    q_ref = refs.pop(0)
    kv_refs = [refs.pop(0) for _ in range(n_kv)]
    kpos_ref = refs.pop(0)
    if not first:
        m_in, a_in = refs.pop(0), refs.pop(0)
    if last:
        o_ref, m_ref, a_ref = refs
    else:
        m_ref, a_ref = refs
    head0, head_count = heads
    block_rows = 32 * head_count
    span = 256 // block_rows
    tiles = CHAINS * span
    keys = sum(r.shape[0] for r in kv_refs) * 32
    per_unit = max(span, 1024 // keys)
    units = 2 if per_unit <= 2 else 1
    per_body = per_unit * units
    rows = [pl.ds(c * 256, 256) for c in range(CHAINS)]

    def query_tile(order):
        parts = []
        for i in range(span):
            x = q_ref[meta[order + i]]
            parts += [x[:, h * HD : (h + 1) * HD] for h in range(head0, head0 + head_count)]
        return jnp.concatenate(parts, axis=0)

    def key_tile(orders):
        ks, vs = [], []
        for order in orders:
            block = meta[order]
            for r in kv_refs:
                kv = r[:, block].reshape(r.shape[0] * 32, 2 * HD)
                ks.append(kv[:, :HD])
                vs.append(kv[:, HD:])
        k = jnp.concatenate(ks, axis=0) if len(ks) > 1 else ks[0]
        v = jnp.concatenate(vs, axis=0) if len(vs) > 1 else vs[0]
        return k, jnp.concatenate([v, jnp.ones_like(v)], axis=1)

    def step(index, carry):
        base = index * tiles
        if last:
            m_at = [m_ref.at[rows[c]] for c in range(CHAINS)]
            a_at = [a_ref.at[rows[c]] for c in range(CHAINS)]
        else:
            m_at = [m_ref.at[base + c] for c in range(CHAINS)]
            a_at = [a_ref.at[base + c] for c in range(CHAINS)]
        for c in range(CHAINS):
            if first:
                m_at[c][...] = jnp.full((256, HD), NEG, f32)
                a_at[c][...] = jnp.zeros((256, 2 * HD), f32)
            elif last:
                for i in range(span):
                    source = pl.ds(32 * head0, block_rows)
                    target = pl.ds(c * 256 + i * block_rows, block_rows)
                    m_ref[target, :] = m_in[base + c * span + i, source, :]
                    a_ref[target, :] = a_in[base + c * span + i, source, :]
        queries = [query_tile(base + c * span) for c in range(CHAINS)]

        def scores(c, tile, masked):
            s = lax.dot_general(queries[c], tile[0], NT, preferred_element_type=f32)
            if masked:
                row = lax.broadcasted_iota(jnp.int32, (256, HD), 0)
                device = meta[16]
                start = (device % 4) * 128 + (device // 16) * 16
                qpos = start + (row // 16 % 2) * 512 + row % 16 + row // block_rows * 1024
                kpos = jnp.concatenate([kpos_ref[...] + i * 1024 for i in range(span)], axis=1)
                own = span * keys
                allowed = jnp.tile(kpos, (256, 1)) <= jnp.tile(qpos, (1, own // HD))
                rest = s.shape[1] - own
                diagonal = jnp.where(allowed, s[:, rest:], NEG)
                s = jnp.concatenate([s[:, :rest], diagonal], axis=1) if rest else diagonal
            return s

        def weigh(c, s):
            before = m_at[c][...]
            peak = jnp.maximum(before, jnp.max(s, axis=1, keepdims=True))
            p = jnp.exp2(s - jnp.tile(peak, (1, s.shape[1] // HD))).astype(bf16)
            m_at[c][...] = peak
            return p, jnp.exp2(before - peak)

        def add(c, p, factor, vext):
            o = jnp.dot(p, vext, preferred_element_type=f32)
            a_at[c][...] = a_at[c][...] * jnp.tile(factor, (1, 2)) + o

        def run(todo):
            ahead = scores(*todo[0])
            pending = None
            for i, (c, tile, _) in enumerate(todo):
                s = ahead
                if i + 1 < len(todo):
                    ahead = scores(*todo[i + 1])
                p, factor = weigh(c, s)
                if pending is not None:
                    add(*pending)
                pending = (c, p, factor, tile[1])
            add(*pending)

        def body(j, carry):
            found = [
                key_tile([j * per_body + u * per_unit + i for i in range(per_unit)])
                for u in range(units)
            ]
            run([(c, t, False) for t in found for c in range(CHAINS)])
            return carry

        lax.fori_loop(0, base // per_body, body, 0)

        todo = []
        for c in range(CHAINS):
            end = (c + 1) * span
            for begin in range(0, end, per_unit):
                stop = min(begin + per_unit, end)
                todo.append((c, key_tile([base + i for i in range(begin, stop)]), stop == end))
        run(todo)

        if last:
            for c in range(CHAINS):
                a = a_at[c][...]
                o = (a[:, :HD] / a[:, HD:]).astype(bf16)
                for i in range(span):
                    block = meta[base + c * span + i]
                    for h in range(head_count):
                        at = i * block_rows + h * 32
                        o_ref[block, :, h * HD : (h + 1) * HD] = o[at : at + 32]
        return carry

    lax.fori_loop(0, 16 // tiles, step, 0)


def attend(meta, q, kvs, kpos, state, heads, name):
    first, last = state is None, heads is not None
    heads = heads or (0, 8)
    operands = [meta, q, *kvs, kpos]
    in_specs = [SMEM] + [VMEM] * (len(operands) - 1)
    aliases = {}
    if not first:
        if not last:
            aliases = {len(operands): 0, len(operands) + 1: 1}
        operands += list(state)
        in_specs += [VMEM, VMEM]
    pieces = sum(x.shape[0] for x in kvs)
    work = 17 * 16 // 2 * 32 * heads[1] * 32 * pieces
    scratch = []
    if last:
        out_shape = jax.ShapeDtypeStruct((16, 32, heads[1] * HD), bf16)
        scratch = [
            pltpu.VMEM((CHAINS * 256, HD), f32),
            pltpu.VMEM((CHAINS * 256, 2 * HD), f32),
        ]
    else:
        out_shape = (
            jax.ShapeDtypeStruct((16, 256, HD), f32),
            jax.ShapeDtypeStruct((16, 256, 2 * HD), f32),
        )
    return pl.pallas_call(
        functools.partial(attend_kernel, n_kv=len(kvs), first=first, last=last, heads=heads),
        out_shape=out_shape,
        in_specs=in_specs,
        out_specs=VMEM if last else (VMEM, VMEM),
        scratch_shapes=scratch,
        input_output_aliases=aliases,
        compiler_params=pltpu.CompilerParams(vmem_limit_bytes=VMEM_LIMIT),
        cost_estimate=pl.CostEstimate(
            flops=work * 1024, bytes_accessed=8 * 2**20, transcendentals=work
        ),
        name=name,
    )(*operands)


def per_device(queries, keys, values, positions, block_order):
    device = lax.axis_index(AXES).astype(jnp.int32)
    order = jnp.arange(16, dtype=jnp.int32)
    inverse = jnp.sum(jnp.where(block_order[None, :] == order[:, None], order[None, :], 0), axis=1)
    meta = jnp.concatenate([inverse.astype(jnp.int32), device[None]])
    offsets = lax.dynamic_index_in_dim(jnp.asarray(KEY_OFFSETS), device, 0, keepdims=True)
    near_at, next_at, far_at = offsets[:, :256], offsets[:, 256:512], offsets[:, 512:]

    def spread(t):
        return lax.all_to_all(t, AXES, 0, 0, axis_index_groups=SPREAD_GROUPS)

    def send(t, perm):
        return lax.ppermute(t, AXES, perm)

    packed = pack(queries, keys, values, positions)
    q = spread(packed.reshape(32, 16, 10 * HD)).reshape(16, 32, 10 * HD)
    own = q[:, :, 8 * HD :]

    line = jnp.stack([own, *[send(own, ring_perm(0, s)) for s in (1, -1, 2)]])
    line_other = send(line, SWAP)
    line_minus, line_plus = send(line, ring_perm(1, 1)), send(line, ring_perm(1, -1))
    state = attend(meta, q, [line, line_other], near_at, None, None, "attend_near")
    line, line_minus, line_plus, state = lax.optimization_barrier(
        (line, line_minus, line_plus, state)
    )
    line_far = send(line, ring_perm(1, 2))
    minus_other, plus_other = send(line_minus, SWAP), send(line_plus, SWAP)
    state = attend(meta, q, [line_minus, line_plus], next_at, state, None, "attend_next")
    line_far, state = lax.optimization_barrier((line_far, state))
    far = [minus_other, plus_other, line_far, send(line_far, SWAP)]
    outs = []
    for half in range(2):
        mixed = attend(meta, q, far, far_at, state, (half * 4, 4), "attend_far")
        outs.append(spread(mixed.reshape(32, 16, 4 * HD)).reshape(8, 4, 16, 4 * HD))
    return unpack(outs)


def solution(mesh):
    return jax.shard_map(
        per_device,
        mesh=mesh,
        in_specs=(P(AXES, None), P(AXES, None), P(AXES, None), P(None, AXES), P()),
        out_specs=P(AXES, None),
        check_vma=False,
    )
```

```python
import functools
import math

import jax
import jax.numpy as jnp
import numpy as np
from jax import lax
from jax.experimental import pallas as pl
from jax.experimental.pallas import tpu as pltpu
from jax.sharding import PartitionSpec as P

HD = 128
ROPE_BASE = 1000000.0
bf16 = jnp.bfloat16
f32 = jnp.float32
AXES = ("blk", "head")
NT = (((1,), (1,)), ((), ()))
NEG = -1e30
CHAINS = 4
VMEM_LIMIT = 24 * 2**20
PACK_LIMIT = 62 * 2**20


def device_id(x, y, z, core):
    return ((x % 2) * 4 + y) * 16 + z * 4 + (x // 2) * 2 + core


COORDS = [(x, y, z, c) for x in range(4) for y in range(4) for z in range(4) for c in range(2)]
SPREAD_GROUPS = [
    [device_id(xh * 2 + b // 4, b % 4, z, c) for b in range(8) for z in range(4)]
    for xh in range(2)
    for c in range(2)
]


def ring_perm(first_axis_core, shift):
    pairs = []
    for x, y, z, c in COORDS:
        if c == first_axis_core:
            target = device_id(x, (y + shift) % 4, z, c)
        else:
            target = device_id((x + shift) % 4, y, z, c)
        pairs.append((device_id(x, y, z, c), target))
    return pairs


SHIFTS = (0, -1, 1, 2)


def row_offsets(x, y, c):
    start = ((x % 4) // 2 * 2 + c) * 128 + ((x % 2) * 4 + y % 4) * 16
    return [start + half * 512 + r for half in range(2) for r in range(16)]


def line_offsets(x, y, c, shift):
    if c == 0:
        return [o for s in SHIFTS for o in row_offsets(x + shift, y + s, c)]
    return [o for s in SHIFTS for o in row_offsets(x + s, y + shift, c)]


def key_offsets(parts):
    table = np.zeros((128, 128 * len(parts)), np.int32)
    for x, y, z, c in COORDS:
        row = [o for shift, own in parts for o in line_offsets(x, y, c if own else 1 - c, shift)]
        table[device_id(x, y, z, c)] = row
    return table


KEY_OFFSETS = key_offsets(
    [(0, True), (0, False)]
    + [(-1, True), (1, True)]
    + [(-1, False), (1, False), (2, True), (2, False)]
)
SWAP = [(device_id(x, y, z, c), device_id(x, y, z, 1 - c)) for x, y, z, c in COORDS]


def rope_tables(pos_ref):
    lane = lax.broadcasted_iota(jnp.int32, (128, HD), 1) % (HD // 2)
    inverse = jnp.exp(lane.astype(f32) * (-2.0 * math.log(ROPE_BASE) / HD))
    columns = [
        jnp.transpose(jnp.broadcast_to(pos_ref[i : i + 1, :].astype(f32), (128, 128)))
        for i in range(3)
    ]
    angles = jnp.where(lane < 16, columns[0], jnp.where(lane < 40, columns[1], columns[2])) * inverse
    upper = lax.broadcasted_iota(jnp.int32, (128, HD), 1) >= HD // 2
    sin = jnp.sin(angles)
    return jnp.cos(angles), jnp.where(upper, sin, -sin)


def rotate(x, cos, sin):
    x = x.astype(f32)
    return (x * cos + pltpu.roll(x, HD // 2, 1) * sin).astype(bf16).reshape(8, 16, HD)


def pack_kv_kernel(k_hbm, v_hbm, pos_hbm, out_ref, cos_ref, sin_ref, k_ref, v_ref, pos_ref, sem):
    copies = [
        pltpu.make_async_copy(source, target, sem.at[i])
        for i, (source, target) in enumerate(((pos_hbm, pos_ref), (k_hbm, k_ref), (v_hbm, v_ref)))
    ]
    for c in copies:
        c.start()
    copies[0].wait()
    cos, sin = rope_tables(pos_ref)
    copies[1].wait()
    copies[2].wait()
    for z in range(4):
        cols = slice(z * HD, (z + 1) * HD)
        out_ref[:, z, :, :HD] = rotate(k_ref[:, cols], cos, sin)
        out_ref[:, z, :, HD:] = v_ref[:, cols].reshape(8, 16, HD)
    fold = math.log2(math.e) / math.sqrt(HD)
    cos_ref[...] = cos * fold
    sin_ref[...] = sin * fold


def pack_q_kernel(q_ref, cos_ref, sin_ref, out_ref):
    cos, sin = cos_ref[...], sin_ref[...]
    for z in range(4):
        for h in range(8):
            col = (z * 8 + h) * HD
            out_ref[:, z, :, h * HD : (h + 1) * HD] = rotate(q_ref[:, col : col + HD], cos, sin)


VMEM = pl.BlockSpec(memory_space=pltpu.VMEM)
HBM = pl.BlockSpec(memory_space=pltpu.HBM)
SMEM = pl.BlockSpec(memory_space=pltpu.SMEM)


def pack_kv(k, v, positions):
    table = jax.ShapeDtypeStruct((128, HD), f32)
    return pl.pallas_call(
        pack_kv_kernel,
        out_shape=(jax.ShapeDtypeStruct((8, 4, 16, 2 * HD), bf16), table, table),
        in_specs=[HBM] * 3,
        out_specs=(VMEM,) * 3,
        scratch_shapes=[
            pltpu.VMEM(k.shape, bf16),
            pltpu.VMEM(v.shape, bf16),
            pltpu.VMEM(positions.shape, jnp.int32),
            pltpu.SemaphoreType.DMA((3,)),
        ],
        compiler_params=pltpu.CompilerParams(vmem_limit_bytes=PACK_LIMIT),
        name="pack_kv",
    )(k, v, positions)


def pack_q(q, cos, sin):
    return pl.pallas_call(
        pack_q_kernel,
        out_shape=jax.ShapeDtypeStruct((8, 4, 16, 8 * HD), bf16),
        in_specs=[VMEM] * 3,
        out_specs=VMEM,
        compiler_params=pltpu.CompilerParams(vmem_limit_bytes=VMEM_LIMIT),
        name="pack_q",
    )(q, cos, sin)


def unpack_kernel(*refs):
    *parts, o_hbm, sem = refs
    width = parts[0].shape[3]
    copies = [
        pltpu.make_async_copy(
            part.at[:, z],
            o_hbm.at[:, :, pl.ds((z * len(parts) + i) * width, width)],
            sem.at[i, z],
        )
        for i, part in enumerate(parts)
        for z in range(4)
    ]
    for c in copies:
        c.start()
    for c in copies:
        c.wait()


def unpack(parts):
    out = pl.pallas_call(
        unpack_kernel,
        out_shape=jax.ShapeDtypeStruct((8, 16, 32 * HD), bf16),
        in_specs=[VMEM] * len(parts),
        out_specs=HBM,
        scratch_shapes=[pltpu.SemaphoreType.DMA((len(parts), 4))],
        compiler_params=pltpu.CompilerParams(vmem_limit_bytes=VMEM_LIMIT),
        name="unpack",
    )(*parts)
    return out.reshape(128, 32 * HD)


def attend_kernel(meta, *refs, n_kv, first, last):
    refs = list(refs)
    q_ref = refs.pop(0)
    kv_refs = [refs.pop(0) for _ in range(n_kv)]
    kpos_ref = refs.pop(0)
    if not first:
        del refs[:2]
    m_ref, a_ref = refs.pop(0), refs.pop(0)
    if last:
        o_ref = refs.pop(0)
    keys = sum(r.shape[0] for r in kv_refs) * 32
    per_unit = max(1, 1024 // keys)
    units = 2 if per_unit <= 2 else 1
    per_body = per_unit * units

    def query_tile(order):
        x = q_ref[meta[order]]
        return jnp.concatenate([x[:, h * HD : (h + 1) * HD] for h in range(8)], axis=0)

    def key_tile(orders):
        ks, vs = [], []
        for order in orders:
            block = meta[order]
            for r in kv_refs:
                kv = r[:, block].reshape(r.shape[0] * 32, 2 * HD)
                ks.append(kv[:, :HD])
                vs.append(kv[:, HD:])
        k = jnp.concatenate(ks, axis=0) if len(ks) > 1 else ks[0]
        v = jnp.concatenate(vs, axis=0) if len(vs) > 1 else vs[0]
        return k, jnp.concatenate([v, jnp.ones_like(v)], axis=1)

    def step(index, carry):
        base = index * CHAINS
        m_at = [m_ref.at[base + c] for c in range(CHAINS)]
        a_at = [a_ref.at[base + c] for c in range(CHAINS)]
        if first:
            for c in range(CHAINS):
                m_at[c][...] = jnp.full((256, HD), NEG, f32)
                a_at[c][...] = jnp.zeros((256, 2 * HD), f32)
        queries = [query_tile(base + c) for c in range(CHAINS)]

        def scores(c, tile, masked):
            s = lax.dot_general(queries[c], tile[0], NT, preferred_element_type=f32)
            if masked:
                row = lax.broadcasted_iota(jnp.int32, (256, HD), 0)
                device = meta[16]
                start = (device % 4) * 128 + (device // 16) * 16
                qpos = start + (row // 16 % 2) * 512 + row % 16
                allowed = jnp.tile(kpos_ref[...], (256, 1)) <= jnp.tile(qpos, (1, keys // HD))
                rest = s.shape[1] - keys
                diagonal = jnp.where(allowed, s[:, rest:], NEG)
                s = jnp.concatenate([s[:, :rest], diagonal], axis=1) if rest else diagonal
            return s

        def weigh(c, s):
            before = m_at[c][...]
            peak = jnp.maximum(before, jnp.max(s, axis=1, keepdims=True))
            p = jnp.exp2(s - jnp.tile(peak, (1, s.shape[1] // HD))).astype(bf16)
            m_at[c][...] = peak
            return p, jnp.exp2(before - peak)

        def add(c, p, factor, vext):
            o = jnp.dot(p, vext, preferred_element_type=f32)
            a_at[c][...] = a_at[c][...] * jnp.tile(factor, (1, 2)) + o

        def run(todo):
            ahead = scores(*todo[0])
            pending = None
            for i, (c, tile, _) in enumerate(todo):
                s = ahead
                if i + 1 < len(todo):
                    ahead = scores(*todo[i + 1])
                p, factor = weigh(c, s)
                if pending is not None:
                    add(*pending)
                pending = (c, p, factor, tile[1])
            add(*pending)

        def body(j, carry):
            found = [
                key_tile([j * per_body + u * per_unit + i for i in range(per_unit)])
                for u in range(units)
            ]
            run([(c, t, False) for t in found for c in range(CHAINS)])
            return carry

        lax.fori_loop(0, base // per_body, body, 0)

        todo = []
        for c in range(CHAINS):
            for begin in range(0, c + 1, per_unit):
                stop = min(begin + per_unit, c + 1)
                todo.append((c, key_tile([base + i for i in range(begin, stop)]), stop == c + 1))
        run(todo)

        if last:
            for c in range(CHAINS):
                a = a_at[c][...]
                o = (a[:, :HD] / a[:, HD:]).astype(bf16)
                block = meta[base + c]
                for h in range(8):
                    o_ref[block, :, h * HD : (h + 1) * HD] = o[h * 32 : (h + 1) * 32]
        return carry

    lax.fori_loop(0, 16 // CHAINS, step, 0)


def attend(meta, q, kvs, kpos, state, last, name):
    operands = [meta, q, *kvs, kpos]
    in_specs = [SMEM] + [VMEM] * (len(operands) - 1)
    aliases = {}
    if state is not None:
        aliases = {len(operands): 0, len(operands) + 1: 1}
        operands += list(state)
        in_specs += [VMEM, VMEM]
    work = 17 * 16 // 2 * 256 * 32 * sum(x.shape[0] for x in kvs)
    out_shape = [
        jax.ShapeDtypeStruct((16, 256, HD), f32),
        jax.ShapeDtypeStruct((16, 256, 2 * HD), f32),
    ]
    if last:
        out_shape.append(jax.ShapeDtypeStruct((16, 32, 8 * HD), bf16))
    return pl.pallas_call(
        functools.partial(attend_kernel, n_kv=len(kvs), first=state is None, last=last),
        out_shape=out_shape,
        in_specs=in_specs,
        out_specs=[VMEM] * len(out_shape),
        input_output_aliases=aliases,
        compiler_params=pltpu.CompilerParams(vmem_limit_bytes=VMEM_LIMIT),
        cost_estimate=pl.CostEstimate(
            flops=work * 1024, bytes_accessed=8 * 2**20, transcendentals=work
        ),
        name=name,
    )(*operands)


def per_device(queries, keys, values, positions, block_order):
    device = lax.axis_index(AXES).astype(jnp.int32)
    order = jnp.arange(16, dtype=jnp.int32)
    inverse = jnp.sum(jnp.where(block_order[None, :] == order[:, None], order[None, :], 0), axis=1)
    meta = jnp.concatenate([inverse.astype(jnp.int32), device[None]])
    offsets = lax.dynamic_index_in_dim(jnp.asarray(KEY_OFFSETS), device, 0, keepdims=True)
    near_at, far_at = offsets[:, :512], offsets[:, 512:]

    def spread(t):
        return lax.all_to_all(t, AXES, 0, 0, axis_index_groups=SPREAD_GROUPS)

    def send(t, perm):
        return lax.ppermute(t, AXES, perm)

    kv_send, cos, sin = pack_kv(keys, values, positions)
    own = spread(kv_send.reshape(32, 16, 2 * HD))
    own, queries = lax.optimization_barrier((own, queries))
    own = own.reshape(16, 32, 2 * HD)
    q_send = pack_q(queries, cos, sin)

    received = [send(own, ring_perm(0, s)) for s in (1, -1, 2)]
    *received, q_send = lax.optimization_barrier((*received, q_send))
    line = jnp.stack([own, *received])
    line_other = send(line, SWAP)
    line_minus, line_plus = send(line, ring_perm(1, 1)), send(line, ring_perm(1, -1))

    line, q_send = lax.optimization_barrier((line, q_send))
    q = spread(q_send.reshape(32, 16, 8 * HD)).reshape(16, 32, 8 * HD)
    q, line, line_other, line_minus, line_plus = lax.optimization_barrier(
        (q, line, line_other, line_minus, line_plus)
    )
    line_far = send(line, ring_perm(1, 2))
    minus_other, plus_other = send(line_minus, SWAP), send(line_plus, SWAP)
    near = [line, line_other, line_minus, line_plus]
    state = attend(meta, q, near, near_at, None, False, "attend_near")
    line_far, minus_other, plus_other, *state = lax.optimization_barrier(
        (line_far, minus_other, plus_other, *state)
    )
    far = [minus_other, plus_other, line_far, send(line_far, SWAP)]
    *_, mixed = attend(meta, q, far, far_at, state, True, "attend_far")
    return unpack([spread(mixed.reshape(32, 16, 8 * HD)).reshape(8, 4, 16, 8 * HD)])


def solution(mesh):
    return jax.shard_map(
        per_device,
        mesh=mesh,
        in_specs=(P(AXES, None), P(AXES, None), P(AXES, None), P(None, AXES), P()),
        out_specs=P(AXES, None),
        check_vma=False,
    )
```

```python
import functools
import math

import jax
import jax.numpy as jnp
import numpy as np
from jax import lax
from jax.experimental import pallas as pl
from jax.experimental.pallas import tpu as pltpu
from jax.sharding import PartitionSpec as P

HD = 128
ROPE_BASE = 1000000.0
bf16 = jnp.bfloat16
f32 = jnp.float32
AXES = ("blk", "head")
NT = (((1,), (1,)), ((), ()))
NEG = -1e30
VMEM_LIMIT = 12 * 2**20
PACK_LIMIT = 62 * 2**20


def device_id(x, y, z, core):
    return ((x % 2) * 4 + y) * 16 + z * 4 + (x // 2) * 2 + core


COORDS = [(x, y, z, c) for x in range(4) for y in range(4) for z in range(4) for c in range(2)]
SPREAD_GROUPS = [
    [device_id(xh * 2 + b // 4, b % 4, z, c) for b in range(8) for z in range(4)]
    for xh in range(2)
    for c in range(2)
]


def ring_perm(first_axis_core, shift):
    pairs = []
    for x, y, z, c in COORDS:
        if c == first_axis_core:
            target = device_id(x, (y + shift) % 4, z, c)
        else:
            target = device_id((x + shift) % 4, y, z, c)
        pairs.append((device_id(x, y, z, c), target))
    return pairs


SHIFTS = (0, -1, 1, 2)


def row_offsets(x, y, c):
    start = ((x % 4) // 2 * 2 + c) * 128 + ((x % 2) * 4 + y % 4) * 16
    return [start + half * 512 + r for half in range(2) for r in range(16)]


def line_offsets(x, y, c, shift):
    if c == 0:
        return [o for s in SHIFTS for o in row_offsets(x + shift, y + s, c)]
    return [o for s in SHIFTS for o in row_offsets(x + s, y + shift, c)]


def key_offsets(parts):
    table = np.zeros((128, 128 * len(parts)), np.int32)
    for x, y, z, c in COORDS:
        row = [o for shift, own in parts for o in line_offsets(x, y, c if own else 1 - c, shift)]
        table[device_id(x, y, z, c)] = row
    return table


KEY_OFFSETS = key_offsets(
    [(0, True), (0, False)]
    + [(-1, True), (1, True)]
    + [(-1, False), (1, False), (2, True), (2, False)]
)
SWAP = [(device_id(x, y, z, c), device_id(x, y, z, 1 - c)) for x, y, z, c in COORDS]


def rope_tables(pos_ref):
    lane = lax.broadcasted_iota(jnp.int32, (128, HD), 1) % (HD // 2)
    inverse = jnp.exp(lane.astype(f32) * (-2.0 * math.log(ROPE_BASE) / HD))
    columns = [
        jnp.transpose(jnp.broadcast_to(pos_ref[i : i + 1, :].astype(f32), (128, 128)))
        for i in range(3)
    ]
    angles = jnp.where(lane < 16, columns[0], jnp.where(lane < 40, columns[1], columns[2])) * inverse
    upper = lax.broadcasted_iota(jnp.int32, (128, HD), 1) >= HD // 2
    sin = jnp.sin(angles)
    return jnp.cos(angles), jnp.where(upper, sin, -sin)


def rotate(x, cos, sin):
    x = x.astype(f32)
    return (x * cos + pltpu.roll(x, HD // 2, 1) * sin).astype(bf16).reshape(8, 16, HD)


def pack_kernel(k_hbm, v_hbm, pos_hbm, q_hbm, kv_out, q_out, k_ref, v_ref, pos_ref, q_ref, sem):
    sources = [(pos_hbm, pos_ref), (k_hbm, k_ref), (v_hbm, v_ref)]
    for z in range(4):
        cols = pl.ds(z * 8 * HD, 8 * HD)
        sources.append((q_hbm.at[:, cols], q_ref.at[:, cols]))
    copies = [pltpu.make_async_copy(*pair, sem.at[i]) for i, pair in enumerate(sources)]
    for c in copies:
        c.start()
    copies[0].wait()
    cos, sin = rope_tables(pos_ref)
    copies[1].wait()
    copies[2].wait()
    for z in range(4):
        cols = slice(z * HD, (z + 1) * HD)
        kv_out[:, z, :, :HD] = rotate(k_ref[:, cols], cos, sin)
        kv_out[:, z, :, HD:] = v_ref[:, cols].reshape(8, 16, HD)
    fold = math.log2(math.e) / math.sqrt(HD)
    cos, sin = cos * fold, sin * fold
    for z in range(4):
        copies[3 + z].wait()
        for h in range(8):
            col = (z * 8 + h) * HD
            q_out[:, z, :, h * HD : (h + 1) * HD] = rotate(q_ref[:, col : col + HD], cos, sin)


VMEM = pl.BlockSpec(memory_space=pltpu.VMEM)
HBM = pl.BlockSpec(memory_space=pltpu.HBM)
SMEM = pl.BlockSpec(memory_space=pltpu.SMEM)


def pack(k, v, positions, q):
    return pl.pallas_call(
        pack_kernel,
        out_shape=(
            jax.ShapeDtypeStruct((8, 4, 16, 2 * HD), bf16),
            jax.ShapeDtypeStruct((8, 4, 16, 8 * HD), bf16),
        ),
        in_specs=[HBM] * 4,
        out_specs=(VMEM, VMEM),
        scratch_shapes=[
            pltpu.VMEM(k.shape, bf16),
            pltpu.VMEM(v.shape, bf16),
            pltpu.VMEM(positions.shape, jnp.int32),
            pltpu.VMEM(q.shape, bf16),
            pltpu.SemaphoreType.DMA((7,)),
        ],
        compiler_params=pltpu.CompilerParams(vmem_limit_bytes=PACK_LIMIT),
        name="pack",
    )(k, v, positions, q)


def unpack_kernel(*refs):
    *parts, o_hbm, sem = refs
    width = parts[0].shape[3]
    copies = [
        pltpu.make_async_copy(
            part.at[:, z],
            o_hbm.at[:, :, pl.ds((z * len(parts) + i) * width, width)],
            sem.at[i, z],
        )
        for i, part in enumerate(parts)
        for z in range(4)
    ]
    for c in copies:
        c.start()
    for c in copies:
        c.wait()


def unpack(parts):
    out = pl.pallas_call(
        unpack_kernel,
        out_shape=jax.ShapeDtypeStruct((8, 16, 32 * HD), bf16),
        in_specs=[VMEM] * len(parts),
        out_specs=HBM,
        scratch_shapes=[pltpu.SemaphoreType.DMA((len(parts), 4))],
        compiler_params=pltpu.CompilerParams(vmem_limit_bytes=VMEM_LIMIT),
        name="unpack",
    )(*parts)
    return out.reshape(128, 32 * HD)


def attend_kernel(meta, *refs, n_kv, offset_at, chains, first, last):
    refs = list(refs)
    q_ref = refs.pop(0)
    kv_refs = [refs.pop(0) for _ in range(n_kv)]
    kpos_ref = refs.pop(0)
    if not first:
        del refs[:2]
    m_ref, a_ref = refs.pop(0), refs.pop(0)
    if last:
        o_ref = refs.pop(0)
    keys = sum(r.shape[0] for r in kv_refs) * 32
    per_unit = max(1, 1024 // keys)
    units = 2 if per_unit <= 2 else 1
    per_body = per_unit * units

    def query_tile(order):
        x = q_ref[meta[order]]
        return jnp.concatenate([x[:, h * HD : (h + 1) * HD] for h in range(8)], axis=0)

    def key_tile(orders):
        ks, vs = [], []
        for order in orders:
            block = meta[order]
            for r in kv_refs:
                kv = r[:, block].reshape(r.shape[0] * 32, 2 * HD)
                ks.append(kv[:, :HD])
                vs.append(kv[:, HD:])
        k = jnp.concatenate(ks, axis=0) if len(ks) > 1 else ks[0]
        v = jnp.concatenate(vs, axis=0) if len(vs) > 1 else vs[0]
        return k, jnp.concatenate([v, jnp.ones_like(v)], axis=1)

    def step(index, carry):
        base = index * chains
        m_at = [m_ref.at[base + c] for c in range(chains)]
        a_at = [a_ref.at[base + c] for c in range(chains)]
        if first:
            for c in range(chains):
                m_at[c][...] = jnp.full((256, HD), NEG, f32)
                a_at[c][...] = jnp.zeros((256, 2 * HD), f32)
        queries = [query_tile(base + c) for c in range(chains)]

        def scores(c, tile, masked):
            s = lax.dot_general(queries[c], tile[0], NT, preferred_element_type=f32)
            if masked:
                row = lax.broadcasted_iota(jnp.int32, (256, HD), 0)
                device = meta[16]
                start = (device % 4) * 128 + (device // 16) * 16
                kpos = kpos_ref[:, offset_at : offset_at + keys]
                qpos = start + (row // 16 % 2) * 512 + row % 16
                allowed = jnp.tile(kpos, (256, 1)) <= jnp.tile(qpos, (1, keys // HD))
                rest = s.shape[1] - keys
                diagonal = jnp.where(allowed, s[:, rest:], NEG)
                s = jnp.concatenate([s[:, :rest], diagonal], axis=1) if rest else diagonal
            return s

        def weigh(c, s):
            before = m_at[c][...]
            peak = jnp.maximum(before, jnp.max(s, axis=1, keepdims=True))
            p = jnp.exp2(s - jnp.tile(peak, (1, s.shape[1] // HD))).astype(bf16)
            m_at[c][...] = peak
            return p, jnp.exp2(before - peak)

        def add(c, p, factor, vext):
            o = jnp.dot(p, vext, preferred_element_type=f32)
            a_at[c][...] = a_at[c][...] * jnp.tile(factor, (1, 2)) + o

        def run(todo):
            ahead = scores(*todo[0])
            pending = None
            for i, (c, tile, _) in enumerate(todo):
                s = ahead
                if i + 1 < len(todo):
                    ahead = scores(*todo[i + 1])
                p, factor = weigh(c, s)
                if pending is not None:
                    add(*pending)
                pending = (c, p, factor, tile[1])
            add(*pending)

        def body(j, carry):
            found = [
                key_tile([j * per_body + u * per_unit + i for i in range(per_unit)])
                for u in range(units)
            ]
            run([(c, t, False) for t in found for c in range(chains)])
            return carry

        lax.fori_loop(0, base // per_body, body, 0)

        todo = []
        for c in range(chains):
            for begin in range(0, c + 1, per_unit):
                stop = min(begin + per_unit, c + 1)
                todo.append((c, key_tile([base + i for i in range(begin, stop)]), stop == c + 1))
        run(todo)

        if last:
            for c in range(chains):
                a = a_at[c][...]
                o = (a[:, :HD] / a[:, HD:]).astype(bf16)
                block = meta[base + c]
                for h in range(8):
                    o_ref[block, :, h * HD : (h + 1) * HD] = o[h * 32 : (h + 1) * 32]
        return carry

    lax.fori_loop(0, 16 // chains, step, 0)


def attend(meta, q, kvs, offsets, offset_at, state, last, chains, name):
    operands = [meta, q, *kvs, offsets]
    in_specs = [SMEM] + [VMEM] * (len(operands) - 1)
    aliases = {}
    if state is not None:
        aliases = {len(operands): 0, len(operands) + 1: 1}
        operands += list(state)
        in_specs += [VMEM, VMEM]
    work = 17 * 16 // 2 * 256 * 32 * sum(x.shape[0] for x in kvs)
    out_shape = [
        jax.ShapeDtypeStruct((16, 256, HD), f32),
        jax.ShapeDtypeStruct((16, 256, 2 * HD), f32),
    ]
    if last:
        out_shape.append(jax.ShapeDtypeStruct((16, 32, 8 * HD), bf16))
    return pl.pallas_call(
        functools.partial(
            attend_kernel,
            n_kv=len(kvs),
            offset_at=offset_at,
            chains=chains,
            first=state is None,
            last=last,
        ),
        out_shape=out_shape,
        in_specs=in_specs,
        out_specs=[VMEM] * len(out_shape),
        input_output_aliases=aliases,
        compiler_params=pltpu.CompilerParams(vmem_limit_bytes=VMEM_LIMIT),
        cost_estimate=pl.CostEstimate(
            flops=work * 1024, bytes_accessed=8 * 2**20, transcendentals=work
        ),
        name=name,
    )(*operands)


def per_device(queries, keys, values, positions, block_order):
    device = lax.axis_index(AXES).astype(jnp.int32)
    order = jnp.arange(16, dtype=jnp.int32)
    inverse = jnp.sum(jnp.where(block_order[None, :] == order[:, None], order[None, :], 0), axis=1)
    meta = jnp.concatenate([inverse.astype(jnp.int32), device[None]])
    offsets = lax.dynamic_index_in_dim(jnp.asarray(KEY_OFFSETS), device, 0, keepdims=True)

    def spread(t):
        return lax.all_to_all(t, AXES, 0, 0, axis_index_groups=SPREAD_GROUPS)

    def send(t, perm):
        return lax.ppermute(t, AXES, perm)

    kv_send, q_send = pack(keys, values, positions, queries)
    own, q_send = lax.optimization_barrier((spread(kv_send.reshape(32, 16, 2 * HD)), q_send))
    own = own.reshape(16, 32, 2 * HD)
    q = spread(q_send.reshape(32, 16, 8 * HD)).reshape(16, 32, 8 * HD)

    received = [send(own, ring_perm(0, s)) for s in (1, -1, 2)]
    *received, q = lax.optimization_barrier((*received, q))
    line = jnp.stack([own, *received])
    line_other = send(line, SWAP)
    line_minus, line_plus = send(line, ring_perm(1, 1)), send(line, ring_perm(1, -1))
    state = attend(meta, q, [line, line_other], offsets, 0, None, False, 8, "attend_near")
    line, line_minus, line_plus, *state = lax.optimization_barrier(
        (line, line_minus, line_plus, *state)
    )
    line_far = send(line, ring_perm(1, 2))
    minus_other, plus_other = send(line_minus, SWAP), send(line_plus, SWAP)
    state = attend(meta, q, [line_minus, line_plus], offsets, 256, state, False, 8, "attend_next")
    line_far, minus_other, plus_other, *state = lax.optimization_barrier(
        (line_far, minus_other, plus_other, *state)
    )
    far = [minus_other, plus_other, line_far, send(line_far, SWAP)]
    *_, mixed = attend(meta, q, far, offsets, 512, state, True, 8, "attend_far")
    return unpack([spread(mixed.reshape(32, 16, 8 * HD)).reshape(8, 4, 16, 8 * HD)])


def solution(mesh):
    return jax.shard_map(
        per_device,
        mesh=mesh,
        in_specs=(P(AXES, None), P(AXES, None), P(AXES, None), P(None, AXES), P()),
        out_specs=P(AXES, None),
        check_vma=False,
    )
```

```python
import functools
import math

import jax
import jax.numpy as jnp
import numpy as np
from jax import lax
from jax.experimental import pallas as pl
from jax.experimental.pallas import tpu as pltpu
from jax.sharding import PartitionSpec as P

HD = 128
ROPE_BASE = 1000000.0
bf16 = jnp.bfloat16
f32 = jnp.float32
AXES = ("blk", "head")
NT = (((1,), (1,)), ((), ()))
NEG = -1e30
VMEM_LIMIT = 24 * 2**20
UNIT_KEYS = 2048
PACK_LIMIT = 62 * 2**20


def device_id(x, y, z, core):
    return ((x % 2) * 4 + y) * 16 + z * 4 + (x // 2) * 2 + core


COORDS = [(x, y, z, c) for x in range(4) for y in range(4) for z in range(4) for c in range(2)]
SPREAD_GROUPS = [
    [device_id(xh * 2 + b // 4, b % 4, z, c) for b in range(8) for z in range(4)]
    for xh in range(2)
    for c in range(2)
]


def ring_perm(first_axis_core, shift):
    pairs = []
    for x, y, z, c in COORDS:
        if c == first_axis_core:
            target = device_id(x, (y + shift) % 4, z, c)
        else:
            target = device_id((x + shift) % 4, y, z, c)
        pairs.append((device_id(x, y, z, c), target))
    return pairs


SHIFTS = (0, -1, 1, 2)


def row_offsets(x, y, c):
    start = ((x % 4) // 2 * 2 + c) * 128 + ((x % 2) * 4 + y % 4) * 16
    return [start + half * 512 + r for half in range(2) for r in range(16)]


def line_offsets(x, y, c, shift):
    if c == 0:
        return [o for s in SHIFTS for o in row_offsets(x + shift, y + s, c)]
    return [o for s in SHIFTS for o in row_offsets(x + s, y + shift, c)]


def key_offsets(parts):
    table = np.zeros((128, 128 * len(parts)), np.int32)
    for x, y, z, c in COORDS:
        row = [o for shift, own in parts for o in line_offsets(x, y, c if own else 1 - c, shift)]
        table[device_id(x, y, z, c)] = row
    return table


KEY_OFFSETS = key_offsets(
    [(0, True), (0, False)]
    + [(-1, True), (1, True)]
    + [(-1, False), (1, False), (2, True), (2, False)]
)
SWAP = [(device_id(x, y, z, c), device_id(x, y, z, 1 - c)) for x, y, z, c in COORDS]


def rope_tables(pos_ref):
    lane = lax.broadcasted_iota(jnp.int32, (128, HD), 1) % (HD // 2)
    inverse = jnp.exp(lane.astype(f32) * (-2.0 * math.log(ROPE_BASE) / HD))
    columns = [
        jnp.transpose(jnp.broadcast_to(pos_ref[i : i + 1, :].astype(f32), (128, 128)))
        for i in range(3)
    ]
    angles = jnp.where(lane < 16, columns[0], jnp.where(lane < 40, columns[1], columns[2])) * inverse
    upper = lax.broadcasted_iota(jnp.int32, (128, HD), 1) >= HD // 2
    sin = jnp.sin(angles)
    return jnp.cos(angles), jnp.where(upper, sin, -sin)


def rotate(x, cos, sin):
    x = x.astype(f32)
    return (x * cos + pltpu.roll(x, HD // 2, 1) * sin).astype(bf16).reshape(8, 16, HD)


def pack_kernel(k_hbm, v_hbm, pos_hbm, q_hbm, kv_out, q_out, k_ref, v_ref, pos_ref, q_ref, sem):
    sources = [(pos_hbm, pos_ref), (k_hbm, k_ref), (v_hbm, v_ref)]
    for z in range(4):
        cols = pl.ds(z * 8 * HD, 8 * HD)
        sources.append((q_hbm.at[:, cols], q_ref.at[:, cols]))
    copies = [pltpu.make_async_copy(*pair, sem.at[i]) for i, pair in enumerate(sources)]
    for c in copies:
        c.start()
    copies[0].wait()
    cos, sin = rope_tables(pos_ref)
    copies[1].wait()
    copies[2].wait()
    for z in range(4):
        cols = slice(z * HD, (z + 1) * HD)
        kv_out[:, z, :, :HD] = rotate(k_ref[:, cols], cos, sin)
        kv_out[:, z, :, HD:] = v_ref[:, cols].reshape(8, 16, HD)
    fold = math.log2(math.e) / math.sqrt(HD)
    cos, sin = cos * fold, sin * fold
    for z in range(4):
        copies[3 + z].wait()
        for h in range(8):
            col = (z * 8 + h) * HD
            q_out[:, z, :, h * HD : (h + 1) * HD] = rotate(q_ref[:, col : col + HD], cos, sin)


VMEM = pl.BlockSpec(memory_space=pltpu.VMEM)
HBM = pl.BlockSpec(memory_space=pltpu.HBM)
SMEM = pl.BlockSpec(memory_space=pltpu.SMEM)


def pack(k, v, positions, q):
    return pl.pallas_call(
        pack_kernel,
        out_shape=(
            jax.ShapeDtypeStruct((8, 4, 16, 2 * HD), bf16),
            jax.ShapeDtypeStruct((8, 4, 16, 8 * HD), bf16),
        ),
        in_specs=[HBM] * 4,
        out_specs=(VMEM, VMEM),
        scratch_shapes=[
            pltpu.VMEM(k.shape, bf16),
            pltpu.VMEM(v.shape, bf16),
            pltpu.VMEM(positions.shape, jnp.int32),
            pltpu.VMEM(q.shape, bf16),
            pltpu.SemaphoreType.DMA((7,)),
        ],
        compiler_params=pltpu.CompilerParams(vmem_limit_bytes=PACK_LIMIT),
        name="pack",
    )(k, v, positions, q)


def unpack_kernel(*refs):
    *parts, o_hbm, sem = refs
    width = parts[0].shape[3]
    copies = [
        pltpu.make_async_copy(
            part.at[:, z],
            o_hbm.at[:, :, pl.ds((z * len(parts) + i) * width, width)],
            sem.at[i, z],
        )
        for i, part in enumerate(parts)
        for z in range(4)
    ]
    for c in copies:
        c.start()
    for c in copies:
        c.wait()


def unpack(parts):
    out = pl.pallas_call(
        unpack_kernel,
        out_shape=jax.ShapeDtypeStruct((8, 16, 32 * HD), bf16),
        in_specs=[VMEM] * len(parts),
        out_specs=HBM,
        scratch_shapes=[pltpu.SemaphoreType.DMA((len(parts), 4))],
        compiler_params=pltpu.CompilerParams(vmem_limit_bytes=VMEM_LIMIT),
        name="unpack",
    )(*parts)
    return out.reshape(128, 32 * HD)


def attend_kernel(meta, *refs, n_kv, offset_at, first, last):
    refs = list(refs)
    q_ref = refs.pop(0)
    kv_refs = [refs.pop(0) for _ in range(n_kv)]
    kpos_ref = refs.pop(0)
    if not first:
        del refs[:2]
    m_ref, a_ref = refs.pop(0), refs.pop(0)
    if last:
        o_ref = refs.pop(0)
    keys = sum(r.shape[0] for r in kv_refs) * 32
    per_unit = max(1, UNIT_KEYS // keys)

    def query_tile(order):
        x = q_ref[meta[order]]
        return jnp.concatenate([x[:, h * HD : (h + 1) * HD] for h in range(8)], axis=0)

    def key_tile(orders):
        ks, vs = [], []
        for order in orders:
            block = meta[order]
            for r in kv_refs:
                kv = r[:, block].reshape(r.shape[0] * 32, 2 * HD)
                ks.append(kv[:, :HD])
                vs.append(kv[:, HD:])
        k = jnp.concatenate(ks, axis=0) if len(ks) > 1 else ks[0]
        v = jnp.concatenate(vs, axis=0) if len(vs) > 1 else vs[0]
        return k, jnp.concatenate([v, jnp.ones_like(v)], axis=1)

    def scores(c, tile, masked):
        s = lax.dot_general(query_tile(c), tile[0], NT, preferred_element_type=f32)
        if masked:
            row = lax.broadcasted_iota(jnp.int32, (256, HD), 0)
            device = meta[16]
            start = (device % 4) * 128 + (device // 16) * 16
            kpos = kpos_ref[:, offset_at : offset_at + keys]
            qpos = start + (row // 16 % 2) * 512 + row % 16
            allowed = jnp.tile(kpos, (256, 1)) <= jnp.tile(qpos, (1, keys // HD))
            rest = s.shape[1] - keys
            diagonal = jnp.where(allowed, s[:, rest:], NEG)
            s = jnp.concatenate([s[:, :rest], diagonal], axis=1) if rest else diagonal
        return s

    peaks = [None] * 16
    sums = [None] * 16

    def weigh(c, s):
        before = m_ref[c] if peaks[c] is None and not first else peaks[c]
        peak = jnp.max(s, axis=1, keepdims=True)
        peak = jnp.broadcast_to(peak, (256, HD)) if before is None else jnp.maximum(before, peak)
        peaks[c] = peak
        p = jnp.exp2(s - jnp.tile(peak, (1, s.shape[1] // HD))).astype(bf16)
        return p, None if before is None else jnp.exp2(before - peak)

    def add(c, p, factor, vext, done):
        o = jnp.dot(p, vext, preferred_element_type=f32)
        if factor is not None:
            o = (a_ref[c] if sums[c] is None else sums[c]) * jnp.tile(factor, (1, 2)) + o
        sums[c] = o
        if done and last:
            o = (o[:, :HD] / o[:, HD:]).astype(bf16)
            block = meta[c]
            for h in range(8):
                o_ref[block, :, h * HD : (h + 1) * HD] = o[h * 32 : (h + 1) * 32]
        elif done:
            m_ref[c] = peaks[c]
            a_ref[c] = o

    todo = []
    for c in range(16):
        for begin in range(0, c + 1, per_unit):
            stop = min(begin + per_unit, c + 1)
            todo.append((c, range(begin, stop), stop == c + 1))

    def start(i):
        c, orders, masked = todo[i]
        tile = key_tile(orders)
        return scores(c, tile, masked), tile[1]

    ahead = start(0)
    pending = None
    for i, (c, _, done) in enumerate(todo):
        s, vext = ahead
        if i + 1 < len(todo):
            ahead = start(i + 1)
        p, factor = weigh(c, s)
        if pending is not None:
            add(*pending)
        pending = (c, p, factor, vext, done)
    add(*pending)


def attend(meta, q, kvs, offsets, offset_at, state, last, name):
    operands = [meta, q, *kvs, offsets]
    in_specs = [SMEM] + [VMEM] * (len(operands) - 1)
    aliases = {}
    if state is not None:
        aliases = {len(operands): 0, len(operands) + 1: 1}
        operands += list(state)
        in_specs += [VMEM, VMEM]
    work = 17 * 16 // 2 * 256 * 32 * sum(x.shape[0] for x in kvs)
    out_shape = [
        jax.ShapeDtypeStruct((16, 256, HD), f32),
        jax.ShapeDtypeStruct((16, 256, 2 * HD), f32),
    ]
    if last:
        out_shape.append(jax.ShapeDtypeStruct((16, 32, 8 * HD), bf16))
    return pl.pallas_call(
        functools.partial(
            attend_kernel,
            n_kv=len(kvs),
            offset_at=offset_at,
            first=state is None,
            last=last,
        ),
        out_shape=out_shape,
        in_specs=in_specs,
        out_specs=[VMEM] * len(out_shape),
        input_output_aliases=aliases,
        compiler_params=pltpu.CompilerParams(vmem_limit_bytes=VMEM_LIMIT),
        cost_estimate=pl.CostEstimate(
            flops=work * 1024, bytes_accessed=8 * 2**20, transcendentals=work
        ),
        name=name,
    )(*operands)


def per_device(queries, keys, values, positions, block_order):
    device = lax.axis_index(AXES).astype(jnp.int32)
    order = jnp.arange(16, dtype=jnp.int32)
    inverse = jnp.sum(jnp.where(block_order[None, :] == order[:, None], order[None, :], 0), axis=1)
    meta = jnp.concatenate([inverse.astype(jnp.int32), device[None]])
    offsets = lax.dynamic_index_in_dim(jnp.asarray(KEY_OFFSETS), device, 0, keepdims=True)

    def spread(t):
        return lax.all_to_all(t, AXES, 0, 0, axis_index_groups=SPREAD_GROUPS)

    def send(t, perm):
        return lax.ppermute(t, AXES, perm)

    kv_send, q_send = pack(keys, values, positions, queries)
    own, q_send = lax.optimization_barrier((spread(kv_send.reshape(32, 16, 2 * HD)), q_send))
    own = own.reshape(16, 32, 2 * HD)
    q = spread(q_send.reshape(32, 16, 8 * HD)).reshape(16, 32, 8 * HD)

    received = [send(own, ring_perm(0, s)) for s in (1, -1, 2)]
    *received, q, meta, offsets = lax.optimization_barrier((*received, q, meta, offsets))
    line = jnp.stack([own, *received])
    line_other = send(line, SWAP)
    line_minus, line_plus = send(line, ring_perm(1, 1)), send(line, ring_perm(1, -1))
    state = attend(meta, q, [line, line_other], offsets, 0, None, False, "attend_near")
    line_minus, line_plus, *state = lax.optimization_barrier((line_minus, line_plus, *state))
    far_a = send(line_minus[:2], ring_perm(1, 1))
    far_b = send(line_plus[2:], ring_perm(1, -1))
    minus_other, plus_other = send(line_minus, SWAP), send(line_plus, SWAP)
    state = attend(meta, q, [line_minus, line_plus], offsets, 256, state, False, "attend_next")
    far_a, far_b, minus_other, plus_other, *state = lax.optimization_barrier(
        (far_a, far_b, minus_other, plus_other, *state)
    )
    far = [minus_other, plus_other, far_a, far_b, send(far_a, SWAP), send(far_b, SWAP)]
    *_, mixed = attend(meta, q, far, offsets, 512, state, True, "attend_far")
    return unpack([spread(mixed.reshape(32, 16, 8 * HD)).reshape(8, 4, 16, 8 * HD)])


def solution(mesh):
    return jax.shard_map(
        per_device,
        mesh=mesh,
        in_specs=(P(AXES, None), P(AXES, None), P(AXES, None), P(None, AXES), P()),
        out_specs=P(AXES, None),
        check_vma=False,
    )
```

```python
import functools
import math

import jax
import jax.numpy as jnp
import numpy as np
from jax import lax
from jax.experimental import pallas as pl
from jax.experimental.pallas import tpu as pltpu
from jax.sharding import PartitionSpec as P

HD = 128
ROPE_BASE = 1000000.0
bf16 = jnp.bfloat16
f32 = jnp.float32
AXES = ("blk", "head")
NT = (((1,), (1,)), ((), ()))
NEG = -1e30
VMEM_LIMIT = 24 * 2**20
UNIT_KEYS = 2048
PACK_LIMIT = 62 * 2**20


def device_id(x, y, z, core):
    return ((x % 2) * 4 + y) * 16 + z * 4 + (x // 2) * 2 + core


COORDS = [(x, y, z, c) for x in range(4) for y in range(4) for z in range(4) for c in range(2)]
SPREAD_GROUPS = [
    [device_id(xh * 2 + b // 4, b % 4, z, c) for b in range(8) for z in range(4)]
    for xh in range(2)
    for c in range(2)
]


def ring_perm(first_axis_core, shift):
    pairs = []
    for x, y, z, c in COORDS:
        if c == first_axis_core:
            target = device_id(x, (y + shift) % 4, z, c)
        else:
            target = device_id((x + shift) % 4, y, z, c)
        pairs.append((device_id(x, y, z, c), target))
    return pairs


SHIFTS = (0, -1, 1, 2)


def row_offsets(x, y, c):
    start = ((x % 4) // 2 * 2 + c) * 128 + ((x % 2) * 4 + y % 4) * 16
    return [start + half * 512 + r for half in range(2) for r in range(16)]


def line_offsets(x, y, c, shift):
    if c == 0:
        return [o for s in SHIFTS for o in row_offsets(x + shift, y + s, c)]
    return [o for s in SHIFTS for o in row_offsets(x + s, y + shift, c)]


def key_offsets(parts):
    table = np.zeros((128, 128 * len(parts)), np.int32)
    for x, y, z, c in COORDS:
        row = [o for shift, own in parts for o in line_offsets(x, y, c if own else 1 - c, shift)]
        table[device_id(x, y, z, c)] = row
    return table


KEY_OFFSETS = key_offsets(
    [(0, True), (0, False)]
    + [(-1, True), (1, True)]
    + [(-1, False), (1, False), (2, True), (2, False)]
)
SWAP = [(device_id(x, y, z, c), device_id(x, y, z, 1 - c)) for x, y, z, c in COORDS]


def rope_tables(pos_ref):
    lane = lax.broadcasted_iota(jnp.int32, (128, HD), 1) % (HD // 2)
    inverse = jnp.exp(lane.astype(f32) * (-2.0 * math.log(ROPE_BASE) / HD))
    columns = [
        jnp.transpose(jnp.broadcast_to(pos_ref[i : i + 1, :].astype(f32), (128, 128)))
        for i in range(3)
    ]
    angles = jnp.where(lane < 16, columns[0], jnp.where(lane < 40, columns[1], columns[2])) * inverse
    upper = lax.broadcasted_iota(jnp.int32, (128, HD), 1) >= HD // 2
    sin = jnp.sin(angles)
    return jnp.cos(angles), jnp.where(upper, sin, -sin)


def rotate(x, cos, sin):
    x = x.astype(f32)
    return (x * cos + pltpu.roll(x, HD // 2, 1) * sin).astype(bf16).reshape(8, 16, HD)


def pack_kernel(k_hbm, v_hbm, pos_hbm, q_hbm, out, k_ref, v_ref, pos_ref, q_ref, sem):
    sources = [(pos_hbm, pos_ref), (k_hbm, k_ref), (v_hbm, v_ref)]
    for z in range(4):
        cols = pl.ds(z * 8 * HD, 8 * HD)
        sources.append((q_hbm.at[:, cols], q_ref.at[:, cols]))
    copies = [pltpu.make_async_copy(*pair, sem.at[i]) for i, pair in enumerate(sources)]
    for c in copies:
        c.start()
    copies[0].wait()
    cos, sin = rope_tables(pos_ref)
    copies[1].wait()
    copies[2].wait()
    for z in range(4):
        cols = slice(z * HD, (z + 1) * HD)
        out[:, z, :, 8 * HD : 9 * HD] = rotate(k_ref[:, cols], cos, sin)
        out[:, z, :, 9 * HD :] = v_ref[:, cols].reshape(8, 16, HD)
    fold = math.log2(math.e) / math.sqrt(HD)
    cos, sin = cos * fold, sin * fold
    for z in range(4):
        copies[3 + z].wait()
        for h in range(8):
            col = (z * 8 + h) * HD
            out[:, z, :, h * HD : (h + 1) * HD] = rotate(q_ref[:, col : col + HD], cos, sin)


VMEM = pl.BlockSpec(memory_space=pltpu.VMEM)
HBM = pl.BlockSpec(memory_space=pltpu.HBM)
SMEM = pl.BlockSpec(memory_space=pltpu.SMEM)


def pack(k, v, positions, q):
    return pl.pallas_call(
        pack_kernel,
        out_shape=jax.ShapeDtypeStruct((8, 4, 16, 10 * HD), bf16),
        in_specs=[HBM] * 4,
        out_specs=VMEM,
        scratch_shapes=[
            pltpu.VMEM(k.shape, bf16),
            pltpu.VMEM(v.shape, bf16),
            pltpu.VMEM(positions.shape, jnp.int32),
            pltpu.VMEM(q.shape, bf16),
            pltpu.SemaphoreType.DMA((7,)),
        ],
        compiler_params=pltpu.CompilerParams(vmem_limit_bytes=PACK_LIMIT),
        name="pack",
    )(k, v, positions, q)


def unpack_kernel(*refs):
    *parts, o_hbm, sem = refs
    width = parts[0].shape[3]
    copies = [
        pltpu.make_async_copy(
            part.at[:, z],
            o_hbm.at[:, :, pl.ds((z * len(parts) + i) * width, width)],
            sem.at[i, z],
        )
        for i, part in enumerate(parts)
        for z in range(4)
    ]
    for c in copies:
        c.start()
    for c in copies:
        c.wait()


def unpack(parts):
    out = pl.pallas_call(
        unpack_kernel,
        out_shape=jax.ShapeDtypeStruct((8, 16, 32 * HD), bf16),
        in_specs=[VMEM] * len(parts),
        out_specs=HBM,
        scratch_shapes=[pltpu.SemaphoreType.DMA((len(parts), 4))],
        compiler_params=pltpu.CompilerParams(vmem_limit_bytes=VMEM_LIMIT),
        name="unpack",
    )(*parts)
    return out.reshape(128, 32 * HD)


def attend_kernel(meta, *refs, n_kv, offset_at, first, last):
    refs = list(refs)
    q_ref = refs.pop(0)
    kv_refs = [refs.pop(0) for _ in range(n_kv)]
    kpos_ref = refs.pop(0)
    if not first:
        del refs[:2]
    m_ref, a_ref = refs.pop(0), refs.pop(0)
    if last:
        o_ref = refs.pop(0)
    keys = sum(r.shape[0] for r in kv_refs) * 32
    per_unit = max(1, UNIT_KEYS // keys)

    def query_tile(order):
        x = q_ref[meta[order]]
        return jnp.concatenate([x[:, h * HD : (h + 1) * HD] for h in range(8)], axis=0)

    def key_tile(orders):
        ks, vs = [], []
        for order in orders:
            block = meta[order]
            for r in kv_refs:
                kv = r[:, block].reshape(r.shape[0] * 32, 2 * HD)
                ks.append(kv[:, :HD])
                vs.append(kv[:, HD:])
        k = jnp.concatenate(ks, axis=0) if len(ks) > 1 else ks[0]
        v = jnp.concatenate(vs, axis=0) if len(vs) > 1 else vs[0]
        return k, jnp.concatenate([v, jnp.ones_like(v)], axis=1)

    def scores(c, tile, masked):
        s = lax.dot_general(query_tile(c), tile[0], NT, preferred_element_type=f32)
        if masked:
            row = lax.broadcasted_iota(jnp.int32, (256, HD), 0)
            device = meta[16]
            start = (device % 4) * 128 + (device // 16) * 16
            kpos = kpos_ref[:, offset_at : offset_at + keys]
            qpos = start + (row // 16 % 2) * 512 + row % 16
            allowed = jnp.tile(kpos, (256, 1)) <= jnp.tile(qpos, (1, keys // HD))
            rest = s.shape[1] - keys
            diagonal = jnp.where(allowed, s[:, rest:], NEG)
            s = jnp.concatenate([s[:, :rest], diagonal], axis=1) if rest else diagonal
        return s

    peaks = [None] * 16
    sums = [None] * 16

    def weigh(c, s):
        before = m_ref[c] if peaks[c] is None and not first else peaks[c]
        peak = jnp.max(s, axis=1, keepdims=True)
        peak = jnp.broadcast_to(peak, (256, HD)) if before is None else jnp.maximum(before, peak)
        peaks[c] = peak
        p = jnp.exp2(s - jnp.tile(peak, (1, s.shape[1] // HD))).astype(bf16)
        return p, None if before is None else jnp.exp2(before - peak)

    def add(c, p, factor, vext, done):
        o = jnp.dot(p, vext, preferred_element_type=f32)
        if factor is not None:
            o = (a_ref[c] if sums[c] is None else sums[c]) * jnp.tile(factor, (1, 2)) + o
        sums[c] = o
        if done and last:
            o = (o[:, :HD] / o[:, HD:]).astype(bf16)
            block = meta[c]
            for h in range(8):
                o_ref[block, :, h * HD : (h + 1) * HD] = o[h * 32 : (h + 1) * 32]
        elif done:
            m_ref[c] = peaks[c]
            a_ref[c] = o

    todo = []
    for c in range(16):
        for begin in range(0, c + 1, per_unit):
            stop = min(begin + per_unit, c + 1)
            todo.append((c, range(begin, stop), stop == c + 1))

    def start(i):
        c, orders, masked = todo[i]
        tile = key_tile(orders)
        return scores(c, tile, masked), tile[1]

    ahead = start(0)
    pending = None
    for i, (c, _, done) in enumerate(todo):
        s, vext = ahead
        if i + 1 < len(todo):
            ahead = start(i + 1)
        p, factor = weigh(c, s)
        if pending is not None:
            add(*pending)
        pending = (c, p, factor, vext, done)
    add(*pending)


def attend(meta, q, kvs, offsets, offset_at, state, last, name):
    operands = [meta, q, *kvs, offsets]
    in_specs = [SMEM] + [VMEM] * (len(operands) - 1)
    aliases = {}
    if state is not None:
        aliases = {len(operands): 0, len(operands) + 1: 1}
        operands += list(state)
        in_specs += [VMEM, VMEM]
    work = 17 * 16 // 2 * 256 * 32 * sum(x.shape[0] for x in kvs)
    out_shape = [
        jax.ShapeDtypeStruct((16, 256, HD), f32),
        jax.ShapeDtypeStruct((16, 256, 2 * HD), f32),
    ]
    if last:
        out_shape.append(jax.ShapeDtypeStruct((16, 32, 8 * HD), bf16))
    return pl.pallas_call(
        functools.partial(
            attend_kernel,
            n_kv=len(kvs),
            offset_at=offset_at,
            first=state is None,
            last=last,
        ),
        out_shape=out_shape,
        in_specs=in_specs,
        out_specs=[VMEM] * len(out_shape),
        input_output_aliases=aliases,
        compiler_params=pltpu.CompilerParams(vmem_limit_bytes=VMEM_LIMIT),
        cost_estimate=pl.CostEstimate(
            flops=work * 1024, bytes_accessed=8 * 2**20, transcendentals=work
        ),
        name=name,
    )(*operands)


def per_device(queries, keys, values, positions, block_order):
    device = lax.axis_index(AXES).astype(jnp.int32)
    order = jnp.arange(16, dtype=jnp.int32)
    inverse = jnp.sum(jnp.where(block_order[None, :] == order[:, None], order[None, :], 0), axis=1)
    meta = jnp.concatenate([inverse.astype(jnp.int32), device[None]])
    offsets = lax.dynamic_index_in_dim(jnp.asarray(KEY_OFFSETS), device, 0, keepdims=True)

    def spread(t):
        return lax.all_to_all(t, AXES, 0, 0, axis_index_groups=SPREAD_GROUPS)

    def send(t, perm):
        return lax.ppermute(t, AXES, perm)

    packed = pack(keys, values, positions, queries)
    gathered = spread(packed.reshape(32, 16, 10 * HD)).reshape(16, 32, 10 * HD)
    q, own = gathered[:, :, : 8 * HD], gathered[:, :, 8 * HD :]

    received = [send(own, ring_perm(0, s)) for s in (1, -1, 2)]
    *received, q, meta, offsets = lax.optimization_barrier((*received, q, meta, offsets))
    line = jnp.stack([own, *received])
    line_other = send(line, SWAP)
    line_minus, line_plus = send(line, ring_perm(1, 1)), send(line, ring_perm(1, -1))
    state = attend(meta, q, [line, line_other], offsets, 0, None, False, "attend_near")
    line_minus, line_plus, *state = lax.optimization_barrier((line_minus, line_plus, *state))
    far_a = send(line_minus[:2], ring_perm(1, 1))
    far_b = send(line_plus[2:], ring_perm(1, -1))
    minus_other, plus_other = send(line_minus, SWAP), send(line_plus, SWAP)
    state = attend(meta, q, [line_minus, line_plus], offsets, 256, state, False, "attend_next")
    far_a, far_b, minus_other, plus_other, *state = lax.optimization_barrier(
        (far_a, far_b, minus_other, plus_other, *state)
    )
    far = [minus_other, plus_other, far_a, far_b, send(far_a, SWAP), send(far_b, SWAP)]
    *_, mixed = attend(meta, q, far, offsets, 512, state, True, "attend_far")
    return unpack([spread(mixed.reshape(32, 16, 8 * HD)).reshape(8, 4, 16, 8 * HD)])


def solution(mesh):
    return jax.shard_map(
        per_device,
        mesh=mesh,
        in_specs=(P(AXES, None), P(AXES, None), P(AXES, None), P(None, AXES), P()),
        out_specs=P(AXES, None),
        check_vma=False,
    )
```
